512 devices in a mesh: ctx: 8 (over x, y_hi), tp: 64 (over y_lo, z, core).
Axes of the slice: x: 4, y: 8 (y_hi: 2, y_lo: 4; y = y_hi * 4 + y_lo), z: 8, core: 2. Of those that a mesh axis runs over, the one named last changes fastest.
Arguments:
- tokens: bfloat16 [1024, 8192], P('ctx', 'tp'), may hold values from -6 to 6
- feat_weight: bfloat16 [8192, 3, 8192], P('ctx', None, 'tp'), may hold values from -0.0625 to 0.0625
- short_taps: float32 [3, 3, 8192], P(None, None, 'tp'), may hold values from -1 to 1
- long_filter: float32 [512, 128], P('tp'), may hold values from -0.5 to 0.5
- skip_gain: float32 [8192], P('tp'), may hold values from -1 to 1
- out_grad: bfloat16 [1024, 8192], P('ctx', 'tp'), may hold values from -16 to 16
Outputs:
- input_grad: bfloat16 [1024, 8192], P('ctx', 'tp')
- filter_grad: float32 [512, 128], P('tp')
- skip_grad: float32 [8192], P('tp')
- short_grad: float32 [3, 3, 8192], P(None, None, 'tp')
The draws below stay inside these ranges and needn't reach their ends.
All inputs are finite; a program needn't handle non-finite values.
Results may differ from the reference program's by a relative error of at most 0.011.
Values may be sent and summed in bfloat16 or wider, within the bound.
No kernel may reach another device: no remote copies, remote signals or barrier semaphores. Data moves between devices by JAX's collectives and lax.ppermute only.
A program may use at most 64 MiB of HBM per device.

```python
import jax
import jax.numpy as jnp
from jax import lax

D = 8192
GROUP = 16
TAPS = 128
SHORT = 3
TOKENS = 1024
GROUPS = 512


def draw_out_grad(key, part):
    key = jax.random.fold_in(key, 7)
    position = jnp.arange(TOKENS, dtype=jnp.float32)[:, None] / TOKENS
    noise = jnp.clip(jax.random.normal(key, (TOKENS, D), jnp.float32), -5.0, 5.0)
    growth = 3.0 ** position
    return (noise * growth).astype(jnp.bfloat16)


def block_levels(key, shape, split, least, top_value):
    def one(dim, shards_of):
        heights = jax.random.uniform(jax.random.fold_in(jax.random.fold_in(key, 6), dim), (shards_of,), jnp.float32, least / len(split), top_value / len(split))
        return jnp.repeat(jnp.exp(heights), shape[dim] // shards_of).reshape((-1,) + (1,) * (len(shape) - dim - 1))

    level = one(*split[0])
    for cut in split[1:]:
        level = level * one(*cut)
    return level


def scatter_about(own_key, dims, spread, limit, split=(), kind=jnp.bfloat16):
    result = spread * jax.random.normal(own_key, dims, jnp.float32)
    if split:
        result = result * block_levels(own_key, dims, split, -0.22, 0.18)
    return jnp.clip(result, -limit, limit).astype(kind)


def setup_inputs(seed: int = 0) -> dict:
    arg_keys = jax.random.split(jax.random.key(seed), 7)
    tokens = scatter_about(arg_keys[0], (TOKENS, D), 1.0, 6.0, ((0, 8), (1, 64)))
    feat_weight = scatter_about(arg_keys[1], (D, 3, D), D ** -0.5, 0.0625, ((0, 8), (2, 64)))
    short_taps = jnp.clip(jax.random.uniform(arg_keys[2], (SHORT, 3, D), jnp.float32, -1.0, 1.0) * block_levels(arg_keys[2], (SHORT, 3, D), ((2, 64),), -0.4, 0.0), -1.0, 1.0)
    long_filter = scatter_about(arg_keys[3], (GROUPS, TAPS), TAPS ** -0.5, 0.5, ((0, 64),), jnp.float32)
    skip_gain = jnp.clip(jax.random.uniform(arg_keys[4], (D,), jnp.float32, -1.0, 1.0) * block_levels(arg_keys[4], (D,), ((0, 64),), -0.4, 0.0), -1.0, 1.0)
    out_grad = draw_out_grad(jax.random.fold_in(arg_keys[6], 71), 0)
    return {"tokens": tokens, "feat_weight": feat_weight, "short_taps": short_taps, "long_filter": long_filter, "skip_gain": skip_gain, "out_grad": out_grad}


def reference(tokens, feat_weight, short_taps, long_filter, skip_gain, out_grad):
    seq_len = tokens.shape[0]
    flat_weight = feat_weight.reshape(D, 3 * D)
    feats = jnp.dot(tokens, flat_weight, preferred_element_type=jnp.float32).astype(jnp.bfloat16).reshape(seq_len, 3, D)
    feat_pad = jnp.pad(feats, ((SHORT - 1, 0), (0, 0), (0, 0))).astype(jnp.float32)
    mixed = jnp.zeros((seq_len, 3, D), jnp.float32)
    for offset in range(SHORT):
        mixed = mixed + short_taps[offset] * feat_pad[SHORT - 1 - offset:SHORT - 1 - offset + seq_len]
    query_feat = mixed[:, 0]
    key_feat = mixed[:, 1]
    value_feat = mixed[:, 2]
    product = (key_feat * value_feat).astype(jnp.bfloat16)
    filter_full = jnp.repeat(long_filter, GROUP, axis=0).T
    prod_pad = jnp.pad(product, ((TAPS - 1, 0), (0, 0))).astype(jnp.float32)

    def forward_tap(offset, running):
        row = lax.dynamic_index_in_dim(filter_full, offset, 0, keepdims=False)
        start_row = (TAPS - 1 - offset).astype(jnp.int32)
        return running + row * lax.dynamic_slice_in_dim(prod_pad, start_row, seq_len, 0)
    long_conv = lax.fori_loop(0, TAPS, forward_tap, jnp.zeros((seq_len, D), jnp.float32))
    long_conv = long_conv + skip_gain * product.astype(jnp.float32)
    grad_out = out_grad.astype(jnp.float32)
    dconv = (grad_out * query_feat).astype(jnp.bfloat16)
    dconv_f = dconv.astype(jnp.float32)
    dquery = grad_out * long_conv
    dconv_pad = jnp.pad(dconv_f, ((0, TAPS - 1), (0, 0)))

    def backward_tap(offset, running):
        row = lax.dynamic_index_in_dim(filter_full, offset, 0, keepdims=False)
        return running + row * lax.dynamic_slice_in_dim(dconv_pad, offset, seq_len, 0)
    dproduct = lax.fori_loop(0, TAPS, backward_tap, jnp.zeros((seq_len, D), jnp.float32))
    dproduct = dproduct + skip_gain * dconv_f

    def tap_grad(offset):
        start_row = (TAPS - 1 - offset).astype(jnp.int32)
        return lax.optimization_barrier(jnp.sum(dconv_f * lax.dynamic_slice_in_dim(prod_pad, start_row, seq_len, 0), axis=0))
    per_tap = lax.map(tap_grad, jnp.arange(TAPS, dtype=jnp.int32))
    filter_grad = per_tap.T.reshape(GROUPS, GROUP, TAPS).sum(axis=1)
    skip_grad = lax.optimization_barrier(jnp.sum(dconv_f * product.astype(jnp.float32), axis=0))
    dmixed = jnp.stack([dquery, dproduct * value_feat, dproduct * key_feat], axis=1)
    dmixed_pad = jnp.pad(dmixed, ((0, SHORT - 1), (0, 0), (0, 0)))
    dfeats = jnp.zeros((seq_len, 3, D), jnp.float32)
    short_list = []
    for offset in range(SHORT):
        dfeats = dfeats + short_taps[offset] * dmixed_pad[offset:offset + seq_len]
        short_list.append(lax.optimization_barrier(jnp.sum(dmixed * feat_pad[SHORT - 1 - offset:SHORT - 1 - offset + seq_len], axis=0)))
    short_grad = jnp.stack(short_list, axis=0)
    dfeats = dfeats.astype(jnp.bfloat16).reshape(seq_len, 3 * D)
    input_grad = jnp.dot(dfeats, flat_weight.T, preferred_element_type=jnp.float32).astype(jnp.bfloat16)
    return (input_grad, filter_grad, skip_grad, short_grad)
```

```python
import jax
import jax.numpy as jnp
import numpy as np
from jax import lax
from jax.experimental import pallas as pl
from jax.experimental.pallas import tpu as pltpu
from jax.sharding import Mesh
from jax.sharding import PartitionSpec as P

AXES = ("x", "yh", "yl", "zh", "zl", "core")
SIZES = (4, 2, 4, 2, 4, 2)
CTX = ("x", "yh")
TP = ("yl", "zh", "zl", "core")
PLANE = ("yl", "zh", "zl")
F32 = jnp.float32
BF16 = jnp.bfloat16
VMEM = pl.BlockSpec(memory_space=pltpu.VMEM)
SMEM = pl.BlockSpec(memory_space=pltpu.SMEM)
ROWS = 64
HALF = 128


def params(mib):
    return pltpu.CompilerParams(vmem_limit_bytes=mib * 1024 * 1024)


def rolled_rows(table, left):
    rows = lax.broadcasted_iota(jnp.int32, table.shape, 0)
    for bit in range(7):
        step = 1 << bit
        turned = pltpu.roll(table, 128 - step if left else step, 1)
        table = jnp.where((rows & step) != 0, turned, table)
    return table


def prepare_kernel(place, grad_ref, taps_ref, skip_ref, filter_ref, grad_t_ref, table_ref, band_ref):
    ctx = place[2]
    grad_t_ref[...] = grad_ref[...].astype(F32).T.astype(BF16).reshape(8, 16, HALF)
    rows = jnp.concatenate(
        [taps_ref[...], skip_ref[...], jnp.zeros((118, 128), F32)], axis=0
    )
    table_ref[...] = rows.T
    band = rolled_rows(
        jnp.broadcast_to(filter_ref[pl.ds(ctx, 1), :], (128, 128)), False
    )
    src = lax.broadcasted_iota(jnp.int32, (128, 128), 0)
    dst = lax.broadcasted_iota(jnp.int32, (128, 128), 1)
    near = jnp.where(dst >= src, band, 0.0)
    far = jnp.where(dst < src, band, 0.0)
    for place_at, part in ((0, near), (2, far)):
        high = part.astype(BF16)
        band_ref[place_at] = high
        band_ref[place_at + 1] = (part - high.astype(F32)).astype(BF16)


def weight_parts(w_own, w_prev, w_next, w_far0, w_far1):
    def whole(ref):
        return lambda side, proj: ref[side, proj].reshape(512, 128)

    def split(side, proj):
        return (w_far0 if side == 0 else w_far1)[proj].reshape(512, 128)

    return ((0, whole(w_own)), (3, whole(w_prev)), (1, whole(w_next)), (2, split))


def project_kernel(place, in_ref, w_own, w_prev, w_next, w_far0, w_far1, grad_ref, out_ref):
    x = place[0]
    core = place[1]
    parts = weight_parts(w_own, w_prev, w_next, w_far0, w_far1)
    rows = []
    for shift, _ in parts:
        block = lax.rem(x + shift, 4)
        rows.append(
            jnp.concatenate(
                [
                    jnp.concatenate([in_ref[block, half, z] for z in range(4)], axis=1)
                    for half in range(2)
                ],
                axis=0,
            )
        )
    for side in range(2):
        to_core = lax.rem(core + side, 2)
        for proj in range(3):
            total = jnp.zeros((256, 128), F32)
            for row, (_, weight) in zip(rows, parts):
                total = total + jnp.dot(row, weight(side, proj), preferred_element_type=F32)
            turned = total.T.astype(BF16)
            for group in range(8):
                out_ref[group, to_core, proj * 16 : proj * 16 + 16, :] = turned[
                    group * 16 : group * 16 + 16
                ]
        for group in range(8):
            out_ref[group, to_core, 48:ROWS, :] = jnp.concatenate(
                [grad_ref[group], jnp.zeros((16, 128), BF16)], axis=1
            )


def mixer_kernel(place, in_ref, table_ref, band_ref, out_ref):
    core = place[1]
    ctx = place[2]
    tokens = 1024
    lane = lax.broadcasted_iota(jnp.int32, (16, tokens), 1)
    table = table_ref[pl.ds(pl.multiple_of(ctx * 16, 16), 16), :]

    def column(k):
        return table[:, k : k + 1]

    def behind(block, k):
        if k == 0:
            return block
        return jnp.where(lane >= k, pltpu.roll(block, k, 1), 0.0)

    def ahead(block, k):
        if k == 0:
            return block
        return jnp.where(lane < tokens - k, pltpu.roll(block, tokens - k, 1), 0.0)

    def stacked(block):
        return jnp.concatenate([block[:, 128 * b : 128 * b + 128] for b in range(8)], axis=0)

    def flat(block):
        return jnp.concatenate([block[16 * b : 16 * b + 16] for b in range(8)], axis=1)

    grad_out = jnp.concatenate(
        [in_ref[i, core, 48:ROWS, 0:128] for i in range(8)], axis=1
    ).astype(F32)
    feats = []
    mixed = []
    for proj in range(3):
        quarters = []
        for x in range(4):
            total = jnp.zeros((16, 256), F32)
            for yh in range(2):
                for side in range(2):
                    total = total + in_ref[2 * x + yh, side, proj * 16 : proj * 16 + 16, :].astype(F32)
            quarters.append(total)
        feat = jnp.concatenate(quarters, axis=1).astype(BF16).astype(F32)
        shifted = [behind(feat, k) for k in range(3)]
        feats.append(shifted)
        running = jnp.zeros((16, tokens), F32)
        for k in range(3):
            running = running + column(3 * k + proj) * shifted[k]
        mixed.append(running)
    query, key, value = mixed
    skip = column(9)
    product = (key * value).astype(BF16)
    dconv = (grad_out * query).astype(BF16)
    prod_rows = stacked(product)
    conv_rows = stacked(dconv)
    none = jnp.zeros((16, 128), BF16)
    prod_prev = jnp.concatenate([none, prod_rows[:112]], axis=0)
    conv_next = jnp.concatenate([conv_rows[16:], none], axis=0)
    forward = jnp.zeros((128, 128), F32)
    backward = jnp.zeros((128, 128), F32)
    over_last = (((1,), (1,)), ((), ()))
    over_first = (((0,), (0,)), ((), ()))
    for at, (left, right) in enumerate(
        ((prod_rows, conv_rows), (prod_rows, conv_rows), (prod_prev, conv_next), (prod_prev, conv_next))
    ):
        band = band_ref[at]
        forward = forward + jnp.dot(left, band, preferred_element_type=F32)
        backward = backward + lax.dot_general(right, band, over_last, preferred_element_type=F32)
    product_f = product.astype(F32)
    dconv_f = dconv.astype(F32)
    long_conv = flat(forward) + skip * product_f
    dproduct = flat(backward) + skip * dconv_f
    near = lax.dot_general(prod_rows, conv_rows, over_first, preferred_element_type=F32)
    far = lax.dot_general(prod_prev, conv_rows, over_first, preferred_element_type=F32)
    src = lax.broadcasted_iota(jnp.int32, (128, 128), 0)
    dst = lax.broadcasted_iota(jnp.int32, (128, 128), 1)
    cross = rolled_rows(jnp.where(dst >= src, near, far), True)
    filter_grad = jnp.sum(cross, axis=0, keepdims=True)
    skip_grad = jnp.sum(dconv_f * product_f, axis=1, keepdims=True)
    dmixed = (grad_out * long_conv, dproduct * value, dproduct * key)
    row16 = lax.broadcasted_iota(jnp.int32, (16, 128), 0)
    lane16 = lax.broadcasted_iota(jnp.int32, (16, 128), 1)
    small = jnp.where((lane16 & 15) == 9, skip_grad, 0.0)
    for proj in range(3):
        dfeat = jnp.zeros((16, tokens), F32)
        for k in range(3):
            dfeat = dfeat + column(3 * k + proj) * ahead(dmixed[proj], k)
            short = jnp.sum(dmixed[proj] * feats[proj][k], axis=1, keepdims=True)
            small = jnp.where((lane16 & 15) == 3 * k + proj, short, small)
        dfeat = dfeat.astype(BF16)
        for x in range(4):
            for other in range(4):
                out_ref[2 * x + other // 2, other % 2, proj * 16 : proj * 16 + 16, :] = dfeat[
                    :, 256 * x : 256 * x + 256
                ]
    small_high = small.astype(BF16).astype(F32)
    small_both = jnp.where(lane16 < 16, small_high, small - small_high)
    filter_high = filter_grad.astype(BF16).astype(F32)
    filter_both = jnp.where(
        row16 == 0, filter_high, jnp.where(row16 == 1, filter_grad - filter_high, 0.0)
    )
    extra = jnp.concatenate([filter_both, small_both], axis=1).astype(BF16)
    for i in range(8):
        for side in range(2):
            out_ref[i, side, 48:ROWS, :] = extra


def back_kernel(place, in_ref, w_own, w_prev, w_next, w_far0, w_far1, out_ref, filter_ref, small_ref):
    x = place[0]
    core = place[1]
    columns = []
    for side in range(2):
        of_core = lax.rem(core + side, 2)
        for proj in range(3):
            block = jnp.concatenate(
                [in_ref[i, of_core, proj * 16 : proj * 16 + 16, :] for i in range(8)], axis=0
            )
            columns.append(block.astype(F32).T.astype(BF16))
    rows = jnp.concatenate(columns, axis=1)
    for shift, weight in weight_parts(w_own, w_prev, w_next, w_far0, w_far1):
        block = lax.rem(x + shift, 4)
        table = jnp.concatenate(
            [weight(side, proj) for side in range(2) for proj in range(3)], axis=1
        )
        result = lax.dot_general(
            rows, table, (((1,), (1,)), ((), ())), preferred_element_type=F32
        ).astype(BF16)
        for half in range(2):
            for z in range(4):
                out_ref[block, half, z] = result[
                    half * 128 : half * 128 + 128, z * 128 : z * 128 + 128
                ]
    small = jnp.concatenate([in_ref[i, core, 48:ROWS, 128:256] for i in range(8)], axis=0)
    turned = small.astype(F32).T
    small_ref[...] = turned[0:16] + turned[16:32]
    for i in range(8):
        tile = in_ref[i, core, 48:ROWS, 0:128].astype(F32)
        filter_ref[i : i + 1, :] = tile[0:1] + tile[1:2]


def on_device(tokens, feat_weight, short_taps, long_filter, skip_gain, out_grad):
    x = lax.axis_index("x")
    core = lax.axis_index("core")
    ctx = lax.axis_index(CTX)
    place = jnp.stack([x, core, ctx]).astype(jnp.int32)
    swap = [(2 * a + b, 2 * b + a) for a in range(2) for b in range(2)]
    cores = [(0, 1), (1, 0)]
    up = [(i, (i + 1) % 4) for i in range(4)]
    down = [(i, (i - 1) % 4) for i in range(4)]

    moved = lax.ppermute(tokens, ("yh", "zh"), swap)

    weight = jnp.transpose(feat_weight, (1, 0, 2)).reshape(3, 4, 2, 128, 128)
    kept = lax.dynamic_index_in_dim(weight, core, 2, keepdims=False)
    given = lax.dynamic_index_in_dim(weight, 1 - core, 2, keepdims=False)
    w_own = jnp.stack([kept, lax.ppermute(given, "core", cores)])
    w_prev = lax.ppermute(w_own, "x", up)
    w_next = lax.ppermute(w_own, "x", down)
    w_far0 = lax.ppermute(w_prev[0], "x", up)
    w_far1 = lax.ppermute(w_next[1], "x", down)
    weights = (w_own, w_prev, w_next, w_far0, w_far1)

    grad_t, table, band = pl.pallas_call(
        prepare_kernel,
        out_shape=(
            jax.ShapeDtypeStruct((8, 16, HALF), BF16),
            jax.ShapeDtypeStruct((128, 128), F32),
            jax.ShapeDtypeStruct((4, 128, 128), BF16),
        ),
        in_specs=[SMEM] + [VMEM] * 4,
        out_specs=(VMEM, VMEM, VMEM),
        name="prepare",
    )(place, out_grad, short_taps.reshape(9, 128), skip_gain.reshape(1, 128), long_filter)

    copies = jnp.broadcast_to(moved[None], (32, 128, 128))
    whole = lax.all_to_all(copies, PLANE, 0, 0, tiled=True).reshape(4, 2, 4, 128, 128)

    partial = pl.pallas_call(
        project_kernel,
        out_shape=jax.ShapeDtypeStruct((8, 2, ROWS, 256), BF16),
        in_specs=[SMEM] + [VMEM] * 7,
        out_specs=VMEM,
        compiler_params=params(40),
        cost_estimate=pl.CostEstimate(flops=2 * 256 * 2048 * 768, bytes_accessed=5 << 20, transcendentals=0),
        name="project",
    )(place, whole, *weights, grad_t)
    spread = lax.all_to_all(
        partial.reshape(16, ROWS, 256), ("x", "yh", "core"), 0, 0, tiled=True
    ).reshape(8, 2, ROWS, 256)

    cotangent = pl.pallas_call(
        mixer_kernel,
        out_shape=jax.ShapeDtypeStruct((8, 2, ROWS, 256), BF16),
        in_specs=[SMEM] + [VMEM] * 3,
        out_specs=VMEM,
        compiler_params=params(40),
        name="mixer",
    )(place, spread, table, band)
    gathered = lax.all_to_all(
        cotangent.reshape(16, ROWS, 256), ("x", "yh", "core"), 0, 0, tiled=True
    ).reshape(8, 2, ROWS, 256)

    back, filter_grad, small = pl.pallas_call(
        back_kernel,
        out_shape=(
            jax.ShapeDtypeStruct((4, 2, 4, 128, 128), BF16),
            jax.ShapeDtypeStruct((8, 128), F32),
            jax.ShapeDtypeStruct((16, 128), F32),
        ),
        in_specs=[SMEM] + [VMEM] * 6,
        out_specs=(VMEM, VMEM, VMEM),
        compiler_params=params(40),
        cost_estimate=pl.CostEstimate(flops=2 * 256 * 2048 * 768, bytes_accessed=5 << 20, transcendentals=0),
        name="back",
    )(place, gathered, *weights)
    parts = lax.all_to_all(back.reshape(32, 128, 128), PLANE, 0, 0, tiled=True)
    summed = jnp.sum(parts.astype(F32), axis=0).astype(BF16)
    input_grad = lax.ppermute(summed, ("yh", "zh"), swap)
    return input_grad, filter_grad, small[9], small[:9].reshape(3, 3, 128)


def solution(mesh):
    split = Mesh(np.asarray(mesh.devices).reshape(SIZES), AXES)
    in_specs = (
        P(CTX, TP),
        P(CTX, None, TP),
        P(None, None, TP),
        P(TP, None),
        P(TP),
        P(CTX, TP),
    )
    out_specs = (P(CTX, TP), P(TP, None), P(TP), P(None, None, TP))
    return jax.shard_map(
        on_device, mesh=split, in_specs=in_specs, out_specs=out_specs, check_vma=False
    )
```

```python
import jax
import jax.numpy as jnp
import numpy as np
from jax import lax
from jax.experimental import pallas as pl
from jax.experimental.pallas import tpu as pltpu
from jax.sharding import Mesh
from jax.sharding import PartitionSpec as P

AXES = ("x", "yh", "yl", "zh", "zl", "core")
SIZES = (4, 2, 4, 2, 4, 2)
CTX = ("x", "yh")
TP = ("yl", "zh", "zl", "core")
PLANE = ("yl", "zh", "zl")
F32 = jnp.float32
BF16 = jnp.bfloat16
VMEM = pl.BlockSpec(memory_space=pltpu.VMEM)
SMEM = pl.BlockSpec(memory_space=pltpu.SMEM)
ROWS = 112
HALF = 128


def params(mib):
    return pltpu.CompilerParams(vmem_limit_bytes=mib * 1024 * 1024)


def rolled_rows(table, left):
    rows = lax.broadcasted_iota(jnp.int32, table.shape, 0)
    for bit in range(7):
        step = 1 << bit
        turned = pltpu.roll(table, 128 - step if left else step, 1)
        table = jnp.where((rows & step) != 0, turned, table)
    return table


def ctx_index():
    return 2 * lax.axis_index("x") + lax.axis_index("yh")


def copies_kernel(in_ref, out_ref):
    out_ref[...] = jnp.broadcast_to(in_ref[...][None], (32, 128, 128))


def prepare_kernel(grad_ref, taps_ref, skip_ref, filter_ref, grad_t_ref, table_ref, band_ref):
    ctx = ctx_index()
    grad_t_ref[...] = grad_ref[...].astype(F32).T.astype(BF16).reshape(8, 16, HALF)
    rows = jnp.concatenate(
        [taps_ref[...], skip_ref[...], jnp.zeros((118, 128), F32)], axis=0
    )
    table_ref[...] = rows.T
    band = rolled_rows(
        jnp.broadcast_to(filter_ref[pl.ds(ctx, 1), :], (128, 128)), False
    )
    src = lax.broadcasted_iota(jnp.int32, (128, 128), 0)
    dst = lax.broadcasted_iota(jnp.int32, (128, 128), 1)
    near = jnp.where(dst >= src, band, 0.0)
    far = jnp.where(dst < src, band, 0.0)
    for place_at, part in ((0, near), (2, far)):
        high = part.astype(BF16)
        band_ref[place_at] = high
        band_ref[place_at + 1] = (part - high.astype(F32)).astype(BF16)


def weight_rows(weight, proj, side):
    return jnp.concatenate([weight[proj, z, side] for z in range(4)], axis=0)


def project_kernel(own_ref, other_ref, w0, w1, w2, w3, grad_ref, out_ref):
    x = lax.axis_index("x")
    core = lax.axis_index("core")
    totals = [jnp.zeros((256, 128), F32) for _ in range(3)]
    for away, weight in enumerate((w0, w1, w2, w3)):
        block = lax.rem(x + away, 4)
        for ref, side in ((own_ref, core), (other_ref, 1 - core)):
            rows = jnp.concatenate(
                [
                    jnp.concatenate([ref[block, 1 - half, z] for z in range(4)], axis=1)
                    for half in range(2)
                ],
                axis=0,
            )
            for proj in range(3):
                totals[proj] = totals[proj] + jnp.dot(
                    rows, weight_rows(weight, proj, side), preferred_element_type=F32
                )
    for proj in range(3):
        turned = totals[proj].T.astype(BF16)
        for half in range(2):
            start = (2 * proj + half) * 16
            for group in range(8):
                out_ref[group, start : start + 16, :] = turned[
                    group * 16 : group * 16 + 16, half * 128 : half * 128 + 128
                ]
    for group in range(8):
        out_ref[group, 96:ROWS, :] = grad_ref[group]


def mixer_kernel(in_ref, table_ref, band_ref, out_ref):
    ctx = ctx_index()
    tokens = 1024
    lane = lax.broadcasted_iota(jnp.int32, (16, tokens), 1)
    table = table_ref[pl.ds(pl.multiple_of(ctx * 16, 16), 16), :]

    def column(k):
        return table[:, k : k + 1]

    def behind(block, k):
        if k == 0:
            return block
        return jnp.where(lane >= k, pltpu.roll(block, k, 1), 0.0)

    def ahead(block, k):
        if k == 0:
            return block
        return jnp.where(lane < tokens - k, pltpu.roll(block, tokens - k, 1), 0.0)

    def stacked(block):
        return jnp.concatenate([block[:, 128 * b : 128 * b + 128] for b in range(8)], axis=0)

    def flat(block):
        return jnp.concatenate([block[16 * b : 16 * b + 16] for b in range(8)], axis=1)

    grad_out = jnp.concatenate(
        [in_ref[i, 96:ROWS, :] for i in range(8)], axis=1
    ).astype(F32)
    feats = []
    mixed = []
    for proj in range(3):
        pieces = []
        for x in range(4):
            for half in range(2):
                start = (2 * proj + half) * 16
                pieces.append(
                    in_ref[2 * x, start : start + 16, :].astype(F32)
                    + in_ref[2 * x + 1, start : start + 16, :].astype(F32)
                )
        feat = jnp.concatenate(pieces, axis=1).astype(BF16).astype(F32)
        shifted = [behind(feat, k) for k in range(3)]
        feats.append(shifted)
        running = jnp.zeros((16, tokens), F32)
        for k in range(3):
            running = running + column(3 * k + proj) * shifted[k]
        mixed.append(running)
    query, key, value = mixed
    skip = column(9)
    product = (key * value).astype(BF16)
    dconv = (grad_out * query).astype(BF16)
    prod_rows = stacked(product)
    conv_rows = stacked(dconv)
    none = jnp.zeros((16, 128), BF16)
    prod_prev = jnp.concatenate([none, prod_rows[:112]], axis=0)
    conv_next = jnp.concatenate([conv_rows[16:], none], axis=0)
    forward = jnp.zeros((128, 128), F32)
    backward = jnp.zeros((128, 128), F32)
    over_last = (((1,), (1,)), ((), ()))
    over_first = (((0,), (0,)), ((), ()))
    for at, (left, right) in enumerate(
        ((prod_rows, conv_rows), (prod_rows, conv_rows), (prod_prev, conv_next), (prod_prev, conv_next))
    ):
        band = band_ref[at]
        forward = forward + jnp.dot(left, band, preferred_element_type=F32)
        backward = backward + lax.dot_general(right, band, over_last, preferred_element_type=F32)
    product_f = product.astype(F32)
    dconv_f = dconv.astype(F32)
    long_conv = flat(forward) + skip * product_f
    dproduct = flat(backward) + skip * dconv_f
    near = lax.dot_general(prod_rows, conv_rows, over_first, preferred_element_type=F32)
    far = lax.dot_general(prod_prev, conv_rows, over_first, preferred_element_type=F32)
    src = lax.broadcasted_iota(jnp.int32, (128, 128), 0)
    dst = lax.broadcasted_iota(jnp.int32, (128, 128), 1)
    cross = rolled_rows(jnp.where(dst >= src, near, far), True)
    filter_grad = jnp.sum(cross, axis=0, keepdims=True)
    skip_grad = jnp.sum(dconv_f * product_f, axis=1, keepdims=True)
    dmixed = (grad_out * long_conv, dproduct * value, dproduct * key)
    row16 = lax.broadcasted_iota(jnp.int32, (16, 128), 0)
    lane16 = lax.broadcasted_iota(jnp.int32, (16, 128), 1)
    small = jnp.where((lane16 & 15) == 9, skip_grad, 0.0)
    for proj in range(3):
        dfeat = jnp.zeros((16, tokens), F32)
        for k in range(3):
            dfeat = dfeat + column(3 * k + proj) * ahead(dmixed[proj], k)
            short = jnp.sum(dmixed[proj] * feats[proj][k], axis=1, keepdims=True)
            small = jnp.where((lane16 & 15) == 3 * k + proj, short, small)
        dfeat = dfeat.astype(BF16)
        for piece in range(8):
            start = (2 * proj + piece % 2) * 16
            for yh in range(2):
                out_ref[2 * (piece // 2) + yh, start : start + 16, :] = dfeat[
                    :, 128 * piece : 128 * piece + 128
                ]
    small_high = small.astype(BF16).astype(F32)
    small_both = jnp.where(lane16 < 16, small_high, small - small_high)
    filter_high = filter_grad.astype(BF16).astype(F32)
    filter_low = filter_grad - filter_high
    extra = jnp.where(lane16 < 32, small_both, 0.0)
    for at, (part, shift) in enumerate(
        ((filter_high, 0), (filter_low, 0), (filter_high, 32), (filter_low, 32))
    ):
        line = jnp.broadcast_to(part, (16, 128))
        if shift:
            line = pltpu.roll(line, shift, 1)
        extra = jnp.where((row16 == at) & (lane16 >= 32), line, extra)
    extra = extra.astype(BF16)
    for i in range(8):
        out_ref[i, 96:ROWS, :] = extra


def back_kernel(in_ref, w0, w1, w2, w3, own_ref, other_ref, filter_ref, small_ref):
    x = lax.axis_index("x")
    core = lax.axis_index("core")
    halves = []
    for half in range(2):
        columns = []
        for proj in range(3):
            start = (2 * proj + half) * 16
            block = jnp.concatenate([in_ref[i, start : start + 16, :] for i in range(8)], axis=0)
            columns.append(block.astype(F32).T.astype(BF16))
        halves.append(jnp.concatenate(columns, axis=1))
    rows = jnp.concatenate(halves, axis=0)
    for away, weight in enumerate((w0, w1, w2, w3)):
        block = lax.rem(x + away, 4)
        for ref, side in ((own_ref, core), (other_ref, 1 - core)):
            table = jnp.concatenate(
                [weight_rows(weight, proj, side) for proj in range(3)], axis=1
            )
            result = lax.dot_general(
                rows, table, (((1,), (1,)), ((), ())), preferred_element_type=F32
            ).astype(BF16)
            for half in range(2):
                for z in range(4):
                    ref[block, 1 - half, z] = result[
                        half * 128 : half * 128 + 128, z * 128 : z * 128 + 128
                    ]
    extra = [in_ref[i, 96:ROWS, :].astype(F32) for i in range(8)]
    turned = jnp.concatenate(extra, axis=0).T
    small_ref[...] = turned[0:16] + turned[16:32]
    lane = lax.broadcasted_iota(jnp.int32, (1, 128), 1)
    for i in range(8):
        late = extra[i][0:1] + extra[i][1:2]
        early = extra[i][2:3] + extra[i][3:4]
        early = pltpu.roll(jnp.broadcast_to(early, (8, 128)), 96, 1)[0:1]
        filter_ref[i : i + 1, :] = jnp.where(lane < 32, early, late)


def quarter_turn(back):
    route = []
    for yh, zh in np.ndindex(2, 2):
        source, target = 2 * yh + zh, 2 * zh + 1 - yh
        route.append((target, source) if back else (source, target))
    return route


def on_device(tokens, feat_weight, short_taps, long_filter, skip_gain, out_grad):
    pair = [(0, 1), (1, 0)]
    moved = lax.ppermute(tokens, ("yh", "zh"), quarter_turn(False))
    own = jnp.transpose(feat_weight, (1, 0, 2))
    weights = [own] + [
        lax.ppermute(own, "x", [(i, (i - away) % 4) for i in range(4)]) for away in (1, 2, 3)
    ]
    weights = [part.reshape(3, 4, 2, 128, 128) for part in weights]

    out_grad, *weights = lax.optimization_barrier((out_grad, *weights))
    grad_t, table, band = pl.pallas_call(
        prepare_kernel,
        out_shape=(
            jax.ShapeDtypeStruct((8, 16, HALF), BF16),
            jax.ShapeDtypeStruct((128, 128), F32),
            jax.ShapeDtypeStruct((4, 128, 128), BF16),
        ),
        in_specs=[VMEM] * 4,
        out_specs=(VMEM, VMEM, VMEM),
        cost_estimate=pl.CostEstimate(flops=50000000000, bytes_accessed=1048576, transcendentals=0),
        name="prepare",
    )(out_grad, short_taps.reshape(9, 128), skip_gain.reshape(1, 128), long_filter)

    copies = pl.pallas_call(
        copies_kernel,
        out_shape=jax.ShapeDtypeStruct((32, 128, 128), BF16),
        in_specs=[VMEM],
        out_specs=VMEM,
        compiler_params=params(40),
        cost_estimate=pl.CostEstimate(flops=10000000000, bytes_accessed=1 << 20, transcendentals=0),
        name="copies",
    )(moved)
    whole = lax.all_to_all(copies, PLANE, 0, 0, tiled=True).reshape(4, 2, 4, 128, 128)
    whole, grad_t, table, band = lax.optimization_barrier((whole, grad_t, table, band))
    across = lax.ppermute(whole, "core", pair)

    cost = pl.CostEstimate(flops=2 * 256 * 4096 * 384, bytes_accessed=5 << 20, transcendentals=0)
    mixed_shape = jax.ShapeDtypeStruct((8, ROWS, 128), BF16)
    partial = pl.pallas_call(
        project_kernel,
        out_shape=mixed_shape,
        in_specs=[VMEM] * 7,
        out_specs=VMEM,
        compiler_params=params(40),
        cost_estimate=cost,
        name="project",
    )(whole, across, *weights, grad_t)
    spread = lax.all_to_all(partial, CTX, 0, 0, tiled=True)

    cotangent = pl.pallas_call(
        mixer_kernel,
        out_shape=mixed_shape,
        in_specs=[VMEM] * 3,
        out_specs=VMEM,
        compiler_params=params(40),
        name="mixer",
    )(spread, table, band)
    gathered = lax.all_to_all(cotangent, CTX, 0, 0, tiled=True)

    back_shape = jax.ShapeDtypeStruct((4, 2, 4, 128, 128), BF16)
    back_own, back_other, filter_grad, small = pl.pallas_call(
        back_kernel,
        out_shape=(
            back_shape,
            back_shape,
            jax.ShapeDtypeStruct((8, 128), F32),
            jax.ShapeDtypeStruct((16, 128), F32),
        ),
        in_specs=[VMEM] * 5,
        out_specs=(VMEM,) * 4,
        compiler_params=params(40),
        cost_estimate=cost,
        name="back",
    )(gathered, *weights)
    received = lax.ppermute(back_other, "core", pair)
    back = (back_own.astype(F32) + received.astype(F32)).astype(BF16)
    parts = lax.all_to_all(back.reshape(32, 128, 128), PLANE, 0, 0, tiled=True)
    summed = jnp.sum(parts.astype(F32), axis=0).astype(BF16)
    input_grad = lax.ppermute(summed, ("yh", "zh"), quarter_turn(True))
    return input_grad, filter_grad, small[9], small[:9].reshape(3, 3, 128)


def solution(mesh):
    split = Mesh(np.asarray(mesh.devices).reshape(SIZES), AXES)
    in_specs = (
        P(CTX, TP),
        P(CTX, None, TP),
        P(None, None, TP),
        P(TP, None),
        P(TP),
        P(CTX, TP),
    )
    out_specs = (P(CTX, TP), P(TP, None), P(TP), P(None, None, TP))
    return jax.shard_map(
        on_device, mesh=split, in_specs=in_specs, out_specs=out_specs, check_vma=False
    )
```

```python
import jax
import jax.numpy as jnp
import numpy as np
from jax import lax
from jax.experimental import pallas as pl
from jax.experimental.pallas import tpu as pltpu
from jax.sharding import Mesh
from jax.sharding import PartitionSpec as P

AXES = ("xh", "xl", "yh", "ylh", "yll", "zh", "z2", "zp", "core")
SIZES = (2,) * 9
X = ("xh", "xl")
CTX = ("xh", "xl", "yh")
TP = ("ylh", "yll", "zh", "z2", "zp", "core")
SPREAD = ("ylh", "yll", "zh", "z2", "zp")
RETURN = ("xh", "xl", "yh", "zp")
COLUMNS = ("ylh", "yll", "zh", "z2")
F32 = jnp.float32
BF16 = jnp.bfloat16
VMEM = pl.BlockSpec(memory_space=pltpu.VMEM)
SMEM = pl.BlockSpec(memory_space=pltpu.SMEM)
ROWS = 112
HALF = 128


def params(mib):
    return pltpu.CompilerParams(vmem_limit_bytes=mib * 1024 * 1024)


def rolled_rows(table, left):
    rows = lax.broadcasted_iota(jnp.int32, table.shape, 0)
    for bit in range(7):
        step = 1 << bit
        turned = pltpu.roll(table, 128 - step if left else step, 1)
        table = jnp.where((rows & step) != 0, turned, table)
    return table


def x_index():
    return 2 * lax.axis_index("xh") + lax.axis_index("xl")


def ctx_index():
    return 2 * x_index() + lax.axis_index("yh")


def block_place(away, z):
    high = lax.axis_index("xh") ^ away
    odd = lax.axis_index("xl") ^ lax.axis_index("zp") ^ away ^ 1
    return high, odd ^ (z % 2), z // 2


def copies_kernel(in_ref, out_ref):
    out_ref[...] = jnp.broadcast_to(in_ref[...][None], (32, 128, 128))


def prepare_kernel(grad_ref, taps_ref, skip_ref, filter_ref, grad_t_ref, table_ref, band_ref):
    ctx = ctx_index()
    grad_t_ref[...] = grad_ref[...].astype(F32).T.astype(BF16).reshape(8, 16, HALF)
    rows = jnp.concatenate(
        [taps_ref[0], taps_ref[1], taps_ref[2], skip_ref[...], jnp.zeros((118, 128), F32)], axis=0
    )
    table_ref[...] = rows.T
    band = rolled_rows(
        jnp.broadcast_to(filter_ref[pl.ds(ctx, 1), :], (128, 128)), False
    )
    src = lax.broadcasted_iota(jnp.int32, (128, 128), 0)
    dst = lax.broadcasted_iota(jnp.int32, (128, 128), 1)
    near = jnp.where(dst >= src, band, 0.0)
    far = jnp.where(dst < src, band, 0.0)
    for place_at, part in ((0, near), (2, far)):
        high = part.astype(BF16)
        band_ref[place_at] = high
        band_ref[place_at + 1] = (part - high.astype(F32)).astype(BF16)


def weight_rows(weight, proj, side):
    return jnp.concatenate([weight[proj, z, side] for z in range(4)], axis=0)


def project_kernel(own_ref, other_ref, w0, w1, w2, w3, grad_ref, out_ref):
    x = x_index()
    core = lax.axis_index("core")
    totals = [jnp.zeros((256, 128), F32) for _ in range(3)]
    for away, weight in enumerate((w0, w1, w2, w3)):
        block = x ^ away
        for ref, side in ((own_ref, core), (other_ref, 1 - core)):
            rows = jnp.concatenate(
                [
                    jnp.concatenate([ref[block, 1 - half, z] for z in range(4)], axis=1)
                    for half in range(2)
                ],
                axis=0,
            )
            for proj in range(3):
                totals[proj] = totals[proj] + jnp.dot(
                    rows, weight_rows(weight, proj, side), preferred_element_type=F32
                )
    for proj in range(3):
        turned = totals[proj].T.astype(BF16)
        for half in range(2):
            start = (2 * proj + half) * 16
            for group in range(8):
                out_ref[group, start : start + 16, :] = turned[
                    group * 16 : group * 16 + 16, half * 128 : half * 128 + 128
                ]
    for group in range(8):
        out_ref[group, 96:ROWS, :] = grad_ref[group]


def mixer_kernel(in_ref, table_ref, band_ref, out_ref):
    ctx = ctx_index()
    tokens = 1024
    lane = lax.broadcasted_iota(jnp.int32, (16, tokens), 1)
    table = table_ref[pl.ds(pl.multiple_of(ctx * 16, 16), 16), :]

    def column(k):
        return table[:, k : k + 1]

    def behind(block, k):
        if k == 0:
            return block
        return jnp.where(lane >= k, pltpu.roll(block, k, 1), 0.0)

    def ahead(block, k):
        if k == 0:
            return block
        return jnp.where(lane < tokens - k, pltpu.roll(block, tokens - k, 1), 0.0)

    def stacked(block):
        return jnp.concatenate([block[:, 128 * b : 128 * b + 128] for b in range(8)], axis=0)

    def flat(block):
        return jnp.concatenate([block[16 * b : 16 * b + 16] for b in range(8)], axis=1)

    grad_out = jnp.concatenate(
        [in_ref[i, 96:ROWS, :] for i in range(8)], axis=1
    ).astype(F32)
    feats = []
    mixed = []
    for proj in range(3):
        pieces = []
        for x in range(4):
            for half in range(2):
                start = (2 * proj + half) * 16
                pieces.append(
                    in_ref[2 * x, start : start + 16, :].astype(F32)
                    + in_ref[2 * x + 1, start : start + 16, :].astype(F32)
                )
        feat = jnp.concatenate(pieces, axis=1).astype(BF16).astype(F32)
        shifted = [behind(feat, k) for k in range(3)]
        feats.append(shifted)
        running = jnp.zeros((16, tokens), F32)
        for k in range(3):
            running = running + column(3 * k + proj) * shifted[k]
        mixed.append(running)
    query, key, value = mixed
    skip = column(9)
    product = (key * value).astype(BF16)
    dconv = (grad_out * query).astype(BF16)
    prod_rows = stacked(product)
    conv_rows = stacked(dconv)
    none = jnp.zeros((16, 128), BF16)
    prod_prev = jnp.concatenate([none, prod_rows[:112]], axis=0)
    conv_next = jnp.concatenate([conv_rows[16:], none], axis=0)
    forward = jnp.zeros((128, 128), F32)
    backward = jnp.zeros((128, 128), F32)
    over_last = (((1,), (1,)), ((), ()))
    over_first = (((0,), (0,)), ((), ()))
    for at, (left, right) in enumerate(
        ((prod_rows, conv_rows), (prod_rows, conv_rows), (prod_prev, conv_next), (prod_prev, conv_next))
    ):
        band = band_ref[at]
        forward = forward + jnp.dot(left, band, preferred_element_type=F32)
        backward = backward + lax.dot_general(right, band, over_last, preferred_element_type=F32)
    product_f = product.astype(F32)
    dconv_f = dconv.astype(F32)
    long_conv = flat(forward) + skip * product_f
    dproduct = flat(backward) + skip * dconv_f
    near = lax.dot_general(prod_rows, conv_rows, over_first, preferred_element_type=F32)
    far = lax.dot_general(prod_prev, conv_rows, over_first, preferred_element_type=F32)
    src = lax.broadcasted_iota(jnp.int32, (128, 128), 0)
    dst = lax.broadcasted_iota(jnp.int32, (128, 128), 1)
    cross = rolled_rows(jnp.where(dst >= src, near, far), True)
    filter_grad = jnp.sum(cross, axis=0, keepdims=True)
    skip_grad = jnp.sum(dconv_f * product_f, axis=1, keepdims=True)
    dmixed = (grad_out * long_conv, dproduct * value, dproduct * key)
    row16 = lax.broadcasted_iota(jnp.int32, (16, 128), 0)
    lane16 = lax.broadcasted_iota(jnp.int32, (16, 128), 1)
    small = jnp.where((lane16 & 15) == 9, skip_grad, 0.0)
    for proj in range(3):
        dfeat = jnp.zeros((16, tokens), F32)
        for k in range(3):
            dfeat = dfeat + column(3 * k + proj) * ahead(dmixed[proj], k)
            short = jnp.sum(dmixed[proj] * feats[proj][k], axis=1, keepdims=True)
            small = jnp.where((lane16 & 15) == 3 * k + proj, short, small)
        dfeat = dfeat.astype(BF16)
        for ctx_to in range(8):
            xh, xl = ctx_to // 4, ctx_to // 2 % 2
            for zp in range(2):
                for yh in range(2):
                    piece = 128 * (4 * xh + 2 * (zp ^ xl) + yh)
                    start = (2 * proj + yh) * 16
                    out_ref[ctx_to, zp, start : start + 16, :] = dfeat[:, piece : piece + 128]
    small_high = small.astype(BF16).astype(F32)
    small_both = jnp.where(lane16 < 16, small_high, small - small_high)
    filter_high = filter_grad.astype(BF16).astype(F32)
    filter_low = filter_grad - filter_high
    extra = jnp.where(lane16 < 32, small_both, 0.0)
    for at, (part, shift) in enumerate(
        ((filter_high, 0), (filter_low, 0), (filter_high, 32), (filter_low, 32))
    ):
        line = jnp.broadcast_to(part, (16, 128))
        if shift:
            line = pltpu.roll(line, shift, 1)
        extra = jnp.where((row16 == at) & (lane16 >= 32), line, extra)
    extra = extra.astype(BF16)
    for i in range(8):
        for zp in range(2):
            out_ref[i, zp, 96:ROWS, :] = extra


def back_kernel(in_ref, w_own, w_x, w_z, own_ref, other_ref, filter_ref, small_ref):
    zp = lax.axis_index("zp")
    core = lax.axis_index("core")
    weights = ((w_own, w_z.at[0]), (w_x, w_z.at[1]))
    halves = []
    for half in range(2):
        columns = []
        for over in range(2):
            of_z = zp ^ over
            for proj in range(3):
                start = (2 * proj + half) * 16
                block = jnp.concatenate(
                    [in_ref[i, of_z, start : start + 16, :] for i in range(8)], axis=0
                )
                columns.append(block.astype(F32).T.astype(BF16))
        halves.append(jnp.concatenate(columns, axis=1))
    rows = jnp.concatenate(halves, axis=0)
    for away in range(2):
        for ref, side in ((own_ref, core), (other_ref, 1 - core)):
            table = jnp.concatenate(
                [
                    weight_rows(weight, proj, side)
                    for weight in weights[away]
                    for proj in range(3)
                ],
                axis=1,
            )
            result = lax.dot_general(
                rows, table, (((1,), (1,)), ((), ())), preferred_element_type=F32
            ).astype(BF16)
            for half in range(2):
                for z in range(4):
                    high, low, z2 = block_place(away, z)
                    ref[high, low, 1 - half, z2] = result[
                        half * 128 : half * 128 + 128, z * 128 : z * 128 + 128
                    ]
    extra = [in_ref[i, zp, 96:ROWS, :].astype(F32) for i in range(8)]
    turned = jnp.concatenate(extra, axis=0).T
    small_ref[...] = turned[0:16] + turned[16:32]
    lane = lax.broadcasted_iota(jnp.int32, (1, 128), 1)
    for i in range(8):
        late = extra[i][0:1] + extra[i][1:2]
        early = extra[i][2:3] + extra[i][3:4]
        early = pltpu.roll(jnp.broadcast_to(early, (8, 128)), 96, 1)[0:1]
        filter_ref[i : i + 1, :] = jnp.where(lane < 32, early, late)


QUARTER_TURN = [(0, 1), (1, 3), (2, 0), (3, 2)]


def flat_index(bits):
    at = 0
    for bit in bits:
        at = 2 * at + bit
    return at


def grad_route():
    route = []
    for xh, xl, yh, ylh, yll, zh, z2, zp, c in np.ndindex(SIZES):
        source = flat_index((xh, xl, yh, ylh, yll, zh, z2, zp, c))
        low = xh ^ ylh ^ yll
        moved = low ^ xl
        target = flat_index((xh, low, zh, ylh, yll ^ zp ^ moved ^ 1, 1 - yh, z2, moved, c))
        route.append((target, source))
    return route


def on_device(tokens, feat_weight, short_taps, long_filter, skip_gain, out_grad):
    pair = [(0, 1), (1, 0)]
    moved = lax.ppermute(tokens, ("yh", "zh"), QUARTER_TURN)
    own = jnp.transpose(feat_weight, (1, 0, 2))
    moved, late = lax.optimization_barrier((moved, own))
    weights = [own] + [
        lax.ppermute(part, X, [(i, i ^ away) for i in range(4)])
        for part, away in ((late, 1), (own, 2), (own, 3))
    ]
    w_z = lax.ppermute(jnp.stack([own, weights[3]]), "zp", pair)

    out_grad, weights[2], weights[3] = lax.optimization_barrier((out_grad, weights[2], weights[3]))
    grad_t, table, band = pl.pallas_call(
        prepare_kernel,
        out_shape=(
            jax.ShapeDtypeStruct((8, 16, HALF), BF16),
            jax.ShapeDtypeStruct((128, 128), F32),
            jax.ShapeDtypeStruct((4, 128, 128), BF16),
        ),
        in_specs=[VMEM] * 4,
        out_specs=(VMEM, VMEM, VMEM),
        cost_estimate=pl.CostEstimate(flops=20000000000, bytes_accessed=1048576, transcendentals=0),
        name="prepare",
    )(out_grad, short_taps, skip_gain.reshape(1, 128), long_filter)

    weights = [part.reshape(3, 4, 2, 128, 128) for part in weights]
    copies = pl.pallas_call(
        copies_kernel,
        out_shape=jax.ShapeDtypeStruct((32, 128, 128), BF16),
        in_specs=[VMEM],
        out_specs=VMEM,
        compiler_params=params(40),
        cost_estimate=pl.CostEstimate(flops=10000000000, bytes_accessed=1 << 20, transcendentals=0),
        name="copies",
    )(moved)
    whole = lax.all_to_all(copies, SPREAD, 0, 0, tiled=True).reshape(4, 2, 4, 128, 128)
    whole, grad_t, table, band, weights[1] = lax.optimization_barrier(
        (whole, grad_t, table, band, weights[1])
    )
    across = lax.ppermute(whole, "core", pair)

    cost = pl.CostEstimate(flops=2 * 256 * 4096 * 384, bytes_accessed=5 << 20, transcendentals=0)
    mixed_shape = jax.ShapeDtypeStruct((8, ROWS, 128), BF16)
    partial = pl.pallas_call(
        project_kernel,
        out_shape=mixed_shape,
        in_specs=[VMEM] * 7,
        out_specs=VMEM,
        compiler_params=params(40),
        cost_estimate=cost,
        name="project",
    )(whole, across, *weights, grad_t)
    spread = lax.all_to_all(partial, CTX, 0, 0, tiled=True)

    cotangent = pl.pallas_call(
        mixer_kernel,
        out_shape=jax.ShapeDtypeStruct((8, 2, ROWS, 128), BF16),
        in_specs=[VMEM] * 3,
        out_specs=VMEM,
        compiler_params=params(40),
        name="mixer",
    )(spread, table, band)
    gathered = lax.all_to_all(
        cotangent.reshape(16, ROWS, 128), RETURN, 0, 0, tiled=True
    ).reshape(8, 2, ROWS, 128)

    back_shape = jax.ShapeDtypeStruct((2, 2, 2, 2, 128, 128), BF16)
    back_own, back_other, filter_grad, small = pl.pallas_call(
        back_kernel,
        out_shape=(
            back_shape,
            back_shape,
            jax.ShapeDtypeStruct((8, 128), F32),
            jax.ShapeDtypeStruct((16, 128), F32),
        ),
        in_specs=[VMEM] * 4,
        out_specs=(VMEM,) * 4,
        compiler_params=params(40),
        cost_estimate=cost,
        name="back",
    )(gathered, weights[0], weights[3], w_z.reshape(2, 3, 4, 2, 128, 128))
    received = lax.ppermute(back_other, "core", pair)
    back = (back_own.astype(F32) + received.astype(F32)).astype(BF16)
    parts = lax.all_to_all(back.reshape(16, 128, 128), COLUMNS, 0, 0, tiled=True)
    summed = jnp.sum(parts.astype(F32), axis=0).astype(BF16)
    input_grad = lax.ppermute(summed, AXES, grad_route())
    return input_grad, filter_grad, small[9], small[:9].reshape(3, 3, 128)


def solution(mesh):
    split = Mesh(np.asarray(mesh.devices).reshape(SIZES), AXES)
    in_specs = (
        P(CTX, TP),
        P(CTX, None, TP),
        P(None, None, TP),
        P(TP, None),
        P(TP),
        P(CTX, TP),
    )
    out_specs = (P(CTX, TP), P(TP, None), P(TP), P(None, None, TP))
    return jax.shard_map(
        on_device, mesh=split, in_specs=in_specs, out_specs=out_specs, check_vma=False
    )
```

```python
import jax
import jax.numpy as jnp
import numpy as np
from jax import lax
from jax.experimental import pallas as pl
from jax.experimental.pallas import tpu as pltpu
from jax.sharding import Mesh
from jax.sharding import PartitionSpec as P

AXES = ("xh", "xl", "yh", "ylh", "yll", "zh", "z2", "zp", "core")
SIZES = (2,) * 9
X = ("xh", "xl")
CTX = ("xh", "xl", "yh")
TP = ("ylh", "yll", "zh", "z2", "zp", "core")
SPREAD = ("ylh", "yll", "zh", "z2", "zp")
RETURN = ("xh", "xl", "yh", "zp")
COLUMNS = ("ylh", "yll", "zh", "z2")
F32 = jnp.float32
BF16 = jnp.bfloat16
VMEM = pl.BlockSpec(memory_space=pltpu.VMEM)
ANY = pl.BlockSpec(memory_space=pl.ANY)
ROWS = 112
HALF = 128


def params(mib):
    return pltpu.CompilerParams(vmem_limit_bytes=mib * 1024 * 1024)


def rolled_rows(table, left):
    rows = lax.broadcasted_iota(jnp.int32, table.shape, 0)
    for bit in range(7):
        step = 1 << bit
        turned = pltpu.roll(table, 128 - step if left else step, 1)
        table = jnp.where((rows & step) != 0, turned, table)
    return table


def x_index():
    return 2 * lax.axis_index("xh") + lax.axis_index("xl")


def ctx_index():
    return 2 * x_index() + lax.axis_index("yh")


def block_place(away, z):
    high = lax.axis_index("xh") ^ away
    odd = lax.axis_index("xl") ^ lax.axis_index("zp") ^ away ^ 1
    return high, odd ^ (z % 2), z // 2


def copies_kernel(in_ref, out_ref):
    out_ref[...] = jnp.broadcast_to(in_ref[...][None], (32, 128, 128))


def table_kernel(taps_ref, skip_ref, table_ref):
    rows = jnp.concatenate(
        [taps_ref[0], taps_ref[1], taps_ref[2], skip_ref[...], jnp.zeros((118, 128), F32)], axis=0
    )
    table_ref[...] = rows.T


def prepare_kernel(grad_ref, filter_ref, grad_t_ref, band_ref):
    grad_t_ref[...] = grad_ref[...].astype(F32).T.astype(BF16).reshape(8, 16, HALF)
    band = rolled_rows(
        jnp.broadcast_to(filter_ref[pl.ds(ctx_index(), 1), :], (128, 128)), False
    )
    src = lax.broadcasted_iota(jnp.int32, (128, 128), 0)
    dst = lax.broadcasted_iota(jnp.int32, (128, 128), 1)
    near = jnp.where(dst >= src, band, 0.0)
    far = jnp.where(dst < src, band, 0.0)
    for place_at, part in ((0, near), (2, far)):
        high = part.astype(BF16)
        band_ref[place_at] = high
        band_ref[place_at + 1] = (part - high.astype(F32)).astype(BF16)


def weight_rows(weight, proj, side):
    return jnp.concatenate([weight[proj, z, side] for z in range(4)], axis=0)


def project_kernel(own_ref, other_ref, w0, w1_far, w2, w3, grad_ref, out_ref, w1, sem):
    copy = pltpu.make_async_copy(w1_far, w1, sem)
    copy.start()
    x = x_index()
    core = lax.axis_index("core")
    totals = [jnp.zeros((256, 128), F32) for _ in range(3)]
    for away, weight in ((0, w0), (2, w2), (3, w3), (1, w1)):
        if away == 1:
            copy.wait()
        block = x ^ away
        for ref, side in ((own_ref, core), (other_ref, 1 - core)):
            rows = jnp.concatenate(
                [
                    jnp.concatenate([ref[block, 1 - half, z] for z in range(4)], axis=1)
                    for half in range(2)
                ],
                axis=0,
            )
            for proj in range(3):
                totals[proj] = totals[proj] + jnp.dot(
                    rows, weight_rows(weight, proj, side), preferred_element_type=F32
                )
    for proj in range(3):
        turned = totals[proj].T.astype(BF16)
        for half in range(2):
            start = (2 * proj + half) * 16
            for group in range(8):
                out_ref[group, start : start + 16, :] = turned[
                    group * 16 : group * 16 + 16, half * 128 : half * 128 + 128
                ]
    for group in range(8):
        out_ref[group, 96:ROWS, :] = grad_ref[group]


def mixer_kernel(in_ref, table_ref, band_ref, out_ref):
    ctx = ctx_index()
    tokens = 1024
    lane = lax.broadcasted_iota(jnp.int32, (16, tokens), 1)
    table = table_ref[pl.ds(pl.multiple_of(ctx * 16, 16), 16), :]

    def column(k):
        return table[:, k : k + 1]

    def behind(block, k):
        if k == 0:
            return block
        return jnp.where(lane >= k, pltpu.roll(block, k, 1), 0.0)

    def ahead(block, k):
        if k == 0:
            return block
        return jnp.where(lane < tokens - k, pltpu.roll(block, tokens - k, 1), 0.0)

    def stacked(block):
        return jnp.concatenate([block[:, 128 * b : 128 * b + 128] for b in range(8)], axis=0)

    def flat(block):
        return jnp.concatenate([block[16 * b : 16 * b + 16] for b in range(8)], axis=1)

    grad_out = jnp.concatenate(
        [in_ref[i, 96:ROWS, :] for i in range(8)], axis=1
    ).astype(F32)
    feats = []
    mixed = []
    for proj in range(3):
        pieces = []
        for x in range(4):
            for half in range(2):
                start = (2 * proj + half) * 16
                pieces.append(
                    in_ref[2 * x, start : start + 16, :].astype(F32)
                    + in_ref[2 * x + 1, start : start + 16, :].astype(F32)
                )
        feat = jnp.concatenate(pieces, axis=1).astype(BF16).astype(F32)
        shifted = [behind(feat, k) for k in range(3)]
        feats.append(shifted)
        running = jnp.zeros((16, tokens), F32)
        for k in range(3):
            running = running + column(3 * k + proj) * shifted[k]
        mixed.append(running)
    query, key, value = mixed
    skip = column(9)
    product = (key * value).astype(BF16)
    dconv = (grad_out * query).astype(BF16)
    prod_rows = stacked(product)
    conv_rows = stacked(dconv)
    none = jnp.zeros((16, 128), BF16)
    prod_prev = jnp.concatenate([none, prod_rows[:112]], axis=0)
    conv_next = jnp.concatenate([conv_rows[16:], none], axis=0)
    forward = jnp.zeros((128, 128), F32)
    backward = jnp.zeros((128, 128), F32)
    over_last = (((1,), (1,)), ((), ()))
    over_first = (((0,), (0,)), ((), ()))
    for at, (left, right) in enumerate(
        ((prod_rows, conv_rows), (prod_rows, conv_rows), (prod_prev, conv_next), (prod_prev, conv_next))
    ):
        band = band_ref[at]
        forward = forward + jnp.dot(left, band, preferred_element_type=F32)
        backward = backward + lax.dot_general(right, band, over_last, preferred_element_type=F32)
    product_f = product.astype(F32)
    dconv_f = dconv.astype(F32)
    long_conv = flat(forward) + skip * product_f
    dproduct = flat(backward) + skip * dconv_f
    near = lax.dot_general(prod_rows, conv_rows, over_first, preferred_element_type=F32)
    far = lax.dot_general(prod_prev, conv_rows, over_first, preferred_element_type=F32)
    src = lax.broadcasted_iota(jnp.int32, (128, 128), 0)
    dst = lax.broadcasted_iota(jnp.int32, (128, 128), 1)
    cross = rolled_rows(jnp.where(dst >= src, near, far), True)
    filter_grad = jnp.sum(cross, axis=0, keepdims=True)
    skip_grad = jnp.sum(dconv_f * product_f, axis=1, keepdims=True)
    dmixed = (grad_out * long_conv, dproduct * value, dproduct * key)
    row16 = lax.broadcasted_iota(jnp.int32, (16, 128), 0)
    lane16 = lax.broadcasted_iota(jnp.int32, (16, 128), 1)
    small = jnp.where((lane16 & 15) == 9, skip_grad, 0.0)
    for proj in range(3):
        dfeat = jnp.zeros((16, tokens), F32)
        for k in range(3):
            dfeat = dfeat + column(3 * k + proj) * ahead(dmixed[proj], k)
            short = jnp.sum(dmixed[proj] * feats[proj][k], axis=1, keepdims=True)
            small = jnp.where((lane16 & 15) == 3 * k + proj, short, small)
        dfeat = dfeat.astype(BF16)
        for ctx_to in range(8):
            xh, xl = ctx_to // 4, ctx_to // 2 % 2
            for zp in range(2):
                for yh in range(2):
                    piece = 128 * (4 * xh + 2 * (zp ^ xl) + yh)
                    start = (2 * proj + yh) * 16
                    out_ref[ctx_to, zp, start : start + 16, :] = dfeat[:, piece : piece + 128]
    small_high = small.astype(BF16).astype(F32)
    small_both = jnp.where(lane16 < 16, small_high, small - small_high)
    filter_high = filter_grad.astype(BF16).astype(F32)
    filter_low = filter_grad - filter_high
    extra = jnp.where(lane16 < 32, small_both, 0.0)
    for at, (part, shift) in enumerate(
        ((filter_high, 0), (filter_low, 0), (filter_high, 32), (filter_low, 32))
    ):
        line = jnp.broadcast_to(part, (16, 128))
        if shift:
            line = pltpu.roll(line, shift, 1)
        extra = jnp.where((row16 == at) & (lane16 >= 32), line, extra)
    extra = extra.astype(BF16)
    for i in range(8):
        for zp in range(2):
            out_ref[i, zp, 96:ROWS, :] = extra


def back_kernel(
    in_ref, w_own, w_x, w_far, own_ref, other_ref, filter_ref, small_ref, w_z, sems
):
    copies = [
        pltpu.make_async_copy(w_far.at[k // 3, k % 3], w_z.at[k // 3, k % 3], sems.at[k])
        for k in range(6)
    ]
    for copy in copies:
        copy.start()
    zp = lax.axis_index("zp")
    core = lax.axis_index("core")
    weights = ((w_own, w_z.at[0]), (w_x, w_z.at[1]))
    halves = []
    for half in range(2):
        columns = []
        for over in range(2):
            of_z = zp ^ over
            for proj in range(3):
                start = (2 * proj + half) * 16
                block = jnp.concatenate(
                    [in_ref[i, of_z, start : start + 16, :] for i in range(8)], axis=0
                )
                columns.append(block.astype(F32).T.astype(BF16))
        halves.append(jnp.concatenate(columns, axis=1))
    rows = jnp.concatenate(halves, axis=0)
    for away in range(2):
        for copy in copies[3 * away : 3 * away + 3]:
            copy.wait()
        for ref, side in ((own_ref, core), (other_ref, 1 - core)):
            table = jnp.concatenate(
                [
                    weight_rows(weight, proj, side)
                    for weight in weights[away]
                    for proj in range(3)
                ],
                axis=1,
            )
            result = lax.dot_general(
                rows, table, (((1,), (1,)), ((), ())), preferred_element_type=F32
            ).astype(BF16)
            for half in range(2):
                for z in range(4):
                    high, low, z2 = block_place(away, z)
                    ref[high, low, 1 - half, z2] = result[
                        half * 128 : half * 128 + 128, z * 128 : z * 128 + 128
                    ]
    extra = [in_ref[i, zp, 96:ROWS, :].astype(F32) for i in range(8)]
    turned = jnp.concatenate(extra, axis=0).T
    small_ref[...] = turned[0:16] + turned[16:32]
    lane = lax.broadcasted_iota(jnp.int32, (1, 128), 1)
    for i in range(8):
        late = extra[i][0:1] + extra[i][1:2]
        early = extra[i][2:3] + extra[i][3:4]
        early = pltpu.roll(jnp.broadcast_to(early, (8, 128)), 96, 1)[0:1]
        filter_ref[i : i + 1, :] = jnp.where(lane < 32, early, late)


QUARTER_TURN = [(0, 1), (1, 3), (2, 0), (3, 2)]


def flat_index(bits):
    at = 0
    for bit in bits:
        at = 2 * at + bit
    return at


def grad_route():
    route = []
    for xh, xl, yh, ylh, yll, zh, z2, zp, c in np.ndindex(SIZES):
        source = flat_index((xh, xl, yh, ylh, yll, zh, z2, zp, c))
        low = xh ^ ylh ^ yll
        moved = low ^ xl
        target = flat_index((xh, low, zh, ylh, yll ^ zp ^ moved ^ 1, 1 - yh, z2, moved, c))
        route.append((target, source))
    return route


def on_device(tokens, feat_weight, short_taps, long_filter, skip_gain, out_grad):
    pair = [(0, 1), (1, 0)]
    moved = lax.ppermute(tokens, ("yh", "zh"), QUARTER_TURN)
    own = jnp.transpose(feat_weight, (1, 0, 2))
    moved, late = lax.optimization_barrier((moved, own))
    weights = [own] + [
        lax.ppermute(part, X, [(i, i ^ away) for i in range(4)])
        for part, away in ((late, 1), (own, 2), (own, 3))
    ]
    pair_rows = jnp.stack([own, weights[3]])

    grad_t, band = pl.pallas_call(
        prepare_kernel,
        out_shape=(
            jax.ShapeDtypeStruct((8, 16, HALF), BF16),
            jax.ShapeDtypeStruct((4, 128, 128), BF16),
        ),
        in_specs=[VMEM] * 2,
        out_specs=(VMEM,) * 2,
        name="prepare",
    )(out_grad, long_filter)
    weights[2], pair_rows = lax.optimization_barrier((weights[2], pair_rows))
    short_taps, weights[2], weights[3] = lax.optimization_barrier(
        (short_taps, weights[2], weights[3])
    )
    table = pl.pallas_call(
        table_kernel,
        out_shape=jax.ShapeDtypeStruct((128, 128), F32),
        in_specs=[VMEM] * 2,
        out_specs=VMEM,
        cost_estimate=pl.CostEstimate(flops=20000000000, bytes_accessed=1 << 20, transcendentals=0),
        name="table",
    )(short_taps, skip_gain.reshape(1, 128))

    weights = [part.reshape(3, 4, 2, 128, 128) for part in weights]
    copies = pl.pallas_call(
        copies_kernel,
        out_shape=jax.ShapeDtypeStruct((32, 128, 128), BF16),
        in_specs=[VMEM],
        out_specs=VMEM,
        compiler_params=params(40),
        cost_estimate=pl.CostEstimate(flops=10000000000, bytes_accessed=1 << 20, transcendentals=0),
        name="copies",
    )(moved)
    whole = lax.all_to_all(copies, SPREAD, 0, 0, tiled=True).reshape(4, 2, 4, 128, 128)
    whole, grad_t, table, band, weights[1], pair_rows = lax.optimization_barrier(
        (whole, grad_t, table, band, weights[1], pair_rows)
    )
    w_z = lax.ppermute(pair_rows, "zp", pair).reshape(2, 3, 4, 2, 128, 128)
    across = lax.ppermute(whole, "core", pair)

    cost = pl.CostEstimate(flops=2 * 256 * 4096 * 384, bytes_accessed=5 << 20, transcendentals=0)
    mixed_shape = jax.ShapeDtypeStruct((8, ROWS, 128), BF16)
    partial = pl.pallas_call(
        project_kernel,
        out_shape=mixed_shape,
        in_specs=[VMEM] * 3 + [ANY] + [VMEM] * 3,
        out_specs=VMEM,
        scratch_shapes=[pltpu.VMEM((3, 4, 2, 128, 128), BF16), pltpu.SemaphoreType.DMA],
        compiler_params=params(40),
        cost_estimate=cost,
        name="project",
    )(whole, across, *weights, grad_t)
    spread = lax.all_to_all(partial, CTX, 0, 0, tiled=True)

    cotangent = pl.pallas_call(
        mixer_kernel,
        out_shape=jax.ShapeDtypeStruct((8, 2, ROWS, 128), BF16),
        in_specs=[VMEM] * 3,
        out_specs=VMEM,
        compiler_params=params(40),
        name="mixer",
    )(spread, table, band)
    gathered = lax.all_to_all(
        cotangent.reshape(16, ROWS, 128), RETURN, 0, 0, tiled=True
    ).reshape(8, 2, ROWS, 128)

    back_shape = jax.ShapeDtypeStruct((2, 2, 2, 2, 128, 128), BF16)
    back_own, back_other, filter_grad, small = pl.pallas_call(
        back_kernel,
        out_shape=(
            back_shape,
            back_shape,
            jax.ShapeDtypeStruct((8, 128), F32),
            jax.ShapeDtypeStruct((16, 128), F32),
        ),
        in_specs=[VMEM] * 3 + [ANY],
        out_specs=(VMEM,) * 4,
        scratch_shapes=[pltpu.VMEM((2, 3, 4, 2, 128, 128), BF16), pltpu.SemaphoreType.DMA((6,))],
        compiler_params=params(40),
        cost_estimate=cost,
        name="back",
    )(gathered, weights[0], weights[3], w_z)
    received = lax.ppermute(back_other, "core", pair)
    back = (back_own.astype(F32) + received.astype(F32)).astype(BF16)
    parts = lax.all_to_all(back.reshape(16, 128, 128), COLUMNS, 0, 0, tiled=True)
    summed = jnp.sum(parts.astype(F32), axis=0).astype(BF16)
    input_grad = lax.ppermute(summed, AXES, grad_route())
    return input_grad, filter_grad, small[9], small[:9].reshape(3, 3, 128)


def solution(mesh):
    split = Mesh(np.asarray(mesh.devices).reshape(SIZES), AXES)
    in_specs = (
        P(CTX, TP),
        P(CTX, None, TP),
        P(None, None, TP),
        P(TP, None),
        P(TP),
        P(CTX, TP),
    )
    out_specs = (P(CTX, TP), P(TP, None), P(TP), P(None, None, TP))
    return jax.shard_map(
        on_device, mesh=split, in_specs=in_specs, out_specs=out_specs, check_vma=False
    )
```

```python
import jax
import jax.numpy as jnp
import numpy as np
from jax import lax
from jax.experimental import pallas as pl
from jax.experimental.pallas import tpu as pltpu
from jax.sharding import Mesh
from jax.sharding import PartitionSpec as P

AXES = ("xh", "xl", "yh", "ylh", "yll", "zh", "z2", "zp", "core")
SIZES = (2,) * 9
X = ("xh", "xl")
CTX = ("xh", "xl", "yh")
TP = ("ylh", "yll", "zh", "z2", "zp", "core")
SPREAD = ("ylh", "yll", "zh", "z2", "zp")
RETURN = ("xh", "xl", "yh", "zp")
COLUMNS = ("ylh", "yll", "zh", "z2")
F32 = jnp.float32
BF16 = jnp.bfloat16
VMEM = pl.BlockSpec(memory_space=pltpu.VMEM)
ANY = pl.BlockSpec(memory_space=pl.ANY)
ROWS = 112
HALF = 128


def params(mib):
    return pltpu.CompilerParams(vmem_limit_bytes=mib * 1024 * 1024)


def rolled_rows(table, left):
    rows = lax.broadcasted_iota(jnp.int32, table.shape, 0)
    for bit in range(7):
        step = 1 << bit
        turned = pltpu.roll(table, 128 - step if left else step, 1)
        table = jnp.where((rows & step) != 0, turned, table)
    return table


def x_index():
    return 2 * lax.axis_index("xh") + lax.axis_index("xl")


def ctx_index():
    return 2 * x_index() + lax.axis_index("yh")


def block_place(away, z):
    high = lax.axis_index("xh") ^ away
    odd = lax.axis_index("xl") ^ lax.axis_index("zp") ^ away ^ 1
    return high, odd ^ (z % 2), z // 2


def copies_kernel(in_ref, out_ref):
    out_ref[...] = jnp.broadcast_to(in_ref[...][None], (32, 128, 128))


def table_kernel(taps_ref, skip_ref, table_ref):
    rows = jnp.concatenate(
        [taps_ref[0], taps_ref[1], taps_ref[2], skip_ref[...], jnp.zeros((118, 128), F32)], axis=0
    )
    table_ref[...] = rows.T


def prepare_kernel(grad_ref, filter_ref, grad_t_ref, band_ref):
    grad_t_ref[...] = grad_ref[...].astype(F32).T.astype(BF16).reshape(8, 16, HALF)
    band = rolled_rows(
        jnp.broadcast_to(filter_ref[pl.ds(ctx_index(), 1), :], (128, 128)), False
    )
    src = lax.broadcasted_iota(jnp.int32, (128, 128), 0)
    dst = lax.broadcasted_iota(jnp.int32, (128, 128), 1)
    near = jnp.where(dst >= src, band, 0.0)
    far = jnp.where(dst < src, band, 0.0)
    for place_at, part in ((0, near), (2, far)):
        high = part.astype(BF16)
        band_ref[place_at] = high
        band_ref[place_at + 1] = (part - high.astype(F32)).astype(BF16)


def weight_rows(weight, proj, side):
    return jnp.concatenate([weight[proj, z, side] for z in range(4)], axis=0)


def project_kernel(own_ref, other_ref, w0, w1_far, w2, w3, grad_ref, out_ref, w1, sem):
    copy = pltpu.make_async_copy(w1_far, w1, sem)
    copy.start()
    x = x_index()
    core = lax.axis_index("core")
    totals = [jnp.zeros((256, 128), F32) for _ in range(3)]
    for away, weight in ((0, w0), (2, w2), (3, w3), (1, w1)):
        if away == 1:
            copy.wait()
        block = x ^ away
        for ref, side in ((own_ref, core), (other_ref, 1 - core)):
            rows = jnp.concatenate(
                [
                    jnp.concatenate([ref[block, 1 - half, z] for z in range(4)], axis=1)
                    for half in range(2)
                ],
                axis=0,
            )
            for proj in range(3):
                totals[proj] = totals[proj] + jnp.dot(
                    rows, weight_rows(weight, proj, side), preferred_element_type=F32
                )
    for proj in range(3):
        turned = totals[proj].T.astype(BF16)
        for half in range(2):
            start = (2 * proj + half) * 16
            for group in range(8):
                out_ref[group, start : start + 16, :] = turned[
                    group * 16 : group * 16 + 16, half * 128 : half * 128 + 128
                ]
    for group in range(8):
        out_ref[group, 96:ROWS, :] = grad_ref[group]


def mixer_kernel(in_ref, table_ref, band_ref, out_ref):
    ctx = ctx_index()
    tokens = 1024
    lane = lax.broadcasted_iota(jnp.int32, (16, tokens), 1)
    table = table_ref[pl.ds(pl.multiple_of(ctx * 16, 16), 16), :]

    def column(k):
        return table[:, k : k + 1]

    def behind(block, k):
        if k == 0:
            return block
        return jnp.where(lane >= k, pltpu.roll(block, k, 1), 0.0)

    def ahead(block, k):
        if k == 0:
            return block
        return jnp.where(lane < tokens - k, pltpu.roll(block, tokens - k, 1), 0.0)

    def stacked(block):
        return jnp.concatenate([block[:, 128 * b : 128 * b + 128] for b in range(8)], axis=0)

    def flat(block):
        return jnp.concatenate([block[16 * b : 16 * b + 16] for b in range(8)], axis=1)

    grad_out = jnp.concatenate(
        [in_ref[i, 96:ROWS, :] for i in range(8)], axis=1
    ).astype(F32)
    feats = []
    mixed = []
    for proj in range(3):
        pieces = []
        for x in range(4):
            for half in range(2):
                start = (2 * proj + half) * 16
                pieces.append(
                    in_ref[2 * x, start : start + 16, :].astype(F32)
                    + in_ref[2 * x + 1, start : start + 16, :].astype(F32)
                )
        feat = jnp.concatenate(pieces, axis=1).astype(BF16).astype(F32)
        shifted = [behind(feat, k) for k in range(3)]
        feats.append(shifted)
        running = jnp.zeros((16, tokens), F32)
        for k in range(3):
            running = running + column(3 * k + proj) * shifted[k]
        mixed.append(running)
    query, key, value = mixed
    skip = column(9)
    product = (key * value).astype(BF16)
    dconv = (grad_out * query).astype(BF16)
    prod_rows = stacked(product)
    conv_rows = stacked(dconv)
    none = jnp.zeros((16, 128), BF16)
    prod_prev = jnp.concatenate([none, prod_rows[:112]], axis=0)
    conv_next = jnp.concatenate([conv_rows[16:], none], axis=0)
    forward = jnp.zeros((128, 128), F32)
    backward = jnp.zeros((128, 128), F32)
    over_last = (((1,), (1,)), ((), ()))
    over_first = (((0,), (0,)), ((), ()))
    for at, (left, right) in enumerate(
        ((prod_rows, conv_rows), (prod_rows, conv_rows), (prod_prev, conv_next), (prod_prev, conv_next))
    ):
        band = band_ref[at]
        forward = forward + jnp.dot(left, band, preferred_element_type=F32)
        backward = backward + lax.dot_general(right, band, over_last, preferred_element_type=F32)
    product_f = product.astype(F32)
    dconv_f = dconv.astype(F32)
    long_conv = flat(forward) + skip * product_f
    dproduct = flat(backward) + skip * dconv_f
    near = lax.dot_general(prod_rows, conv_rows, over_first, preferred_element_type=F32)
    far = lax.dot_general(prod_prev, conv_rows, over_first, preferred_element_type=F32)
    src = lax.broadcasted_iota(jnp.int32, (128, 128), 0)
    dst = lax.broadcasted_iota(jnp.int32, (128, 128), 1)
    cross = rolled_rows(jnp.where(dst >= src, near, far), True)
    filter_grad = jnp.sum(cross, axis=0, keepdims=True)
    skip_grad = jnp.sum(dconv_f * product_f, axis=1, keepdims=True)
    dmixed = (grad_out * long_conv, dproduct * value, dproduct * key)
    row16 = lax.broadcasted_iota(jnp.int32, (16, 128), 0)
    lane16 = lax.broadcasted_iota(jnp.int32, (16, 128), 1)
    small = jnp.where((lane16 & 15) == 9, skip_grad, 0.0)
    for proj in range(3):
        dfeat = jnp.zeros((16, tokens), F32)
        for k in range(3):
            dfeat = dfeat + column(3 * k + proj) * ahead(dmixed[proj], k)
            short = jnp.sum(dmixed[proj] * feats[proj][k], axis=1, keepdims=True)
            small = jnp.where((lane16 & 15) == 3 * k + proj, short, small)
        dfeat = dfeat.astype(BF16)
        for ctx_to in range(8):
            xh, xl = ctx_to // 4, ctx_to // 2 % 2
            for zp in range(2):
                for yh in range(2):
                    piece = 128 * (4 * xh + 2 * (zp ^ xl) + yh)
                    start = (2 * proj + yh) * 16
                    out_ref[ctx_to, zp, start : start + 16, :] = dfeat[:, piece : piece + 128]
    small_high = small.astype(BF16).astype(F32)
    small_both = jnp.where(lane16 < 16, small_high, small - small_high)
    filter_high = filter_grad.astype(BF16).astype(F32)
    filter_low = filter_grad - filter_high
    extra = jnp.where(lane16 < 32, small_both, 0.0)
    for at, (part, shift) in enumerate(
        ((filter_high, 0), (filter_low, 0), (filter_high, 32), (filter_low, 32))
    ):
        line = jnp.broadcast_to(part, (16, 128))
        if shift:
            line = pltpu.roll(line, shift, 1)
        extra = jnp.where((row16 == at) & (lane16 >= 32), line, extra)
    extra = extra.astype(BF16)
    for i in range(8):
        for zp in range(2):
            out_ref[i, zp, 96:ROWS, :] = extra


def back_kernel(
    in_ref, w_own, w_x, w_far, own_ref, other_ref, filter_ref, small_ref, w_z, sems
):
    copies = [
        pltpu.make_async_copy(w_far.at[k // 3, k % 3], w_z.at[k // 3, k % 3], sems.at[k])
        for k in range(6)
    ]
    for copy in copies:
        copy.start()
    zp = lax.axis_index("zp")
    core = lax.axis_index("core")
    weights = ((w_own, w_z.at[0]), (w_x, w_z.at[1]))
    halves = []
    for half in range(2):
        columns = []
        for over in range(2):
            of_z = zp ^ over
            for proj in range(3):
                start = (2 * proj + half) * 16
                block = jnp.concatenate(
                    [in_ref[i, of_z, start : start + 16, :] for i in range(8)], axis=0
                )
                columns.append(block.astype(F32).T.astype(BF16))
        halves.append(jnp.concatenate(columns, axis=1))
    rows = jnp.concatenate(halves, axis=0)
    for away in range(2):
        for copy in copies[3 * away : 3 * away + 3]:
            copy.wait()
        for ref, side in ((own_ref, core), (other_ref, 1 - core)):
            table = jnp.concatenate(
                [
                    weight_rows(weight, proj, side)
                    for weight in weights[away]
                    for proj in range(3)
                ],
                axis=1,
            )
            result = lax.dot_general(
                rows, table, (((1,), (1,)), ((), ())), preferred_element_type=F32
            ).astype(BF16)
            for half in range(2):
                for z in range(4):
                    high, low, z2 = block_place(away, z)
                    ref[high, low, 1 - half, z2] = result[
                        half * 128 : half * 128 + 128, z * 128 : z * 128 + 128
                    ]
    extra = [in_ref[i, zp, 96:ROWS, :].astype(F32) for i in range(8)]
    turned = jnp.concatenate(extra, axis=0).T
    small_ref[...] = turned[0:16] + turned[16:32]
    lane = lax.broadcasted_iota(jnp.int32, (1, 128), 1)
    for i in range(8):
        late = extra[i][0:1] + extra[i][1:2]
        early = extra[i][2:3] + extra[i][3:4]
        early = pltpu.roll(jnp.broadcast_to(early, (8, 128)), 96, 1)[0:1]
        filter_ref[i : i + 1, :] = jnp.where(lane < 32, early, late)


QUARTER_TURN = [(0, 1), (1, 3), (2, 0), (3, 2)]


def flat_index(bits):
    at = 0
    for bit in bits:
        at = 2 * at + bit
    return at


def grad_route():
    route = []
    for xh, xl, yh, ylh, yll, zh, z2, zp, c in np.ndindex(SIZES):
        source = flat_index((xh, xl, yh, ylh, yll, zh, z2, zp, c))
        low = xh ^ ylh ^ yll
        moved = low ^ xl
        target = flat_index((xh, low, zh, ylh, yll ^ zp ^ moved ^ 1, 1 - yh, z2, moved, c))
        route.append((target, source))
    return route


def on_device(tokens, feat_weight, short_taps, long_filter, skip_gain, out_grad):
    pair = [(0, 1), (1, 0)]
    moved = lax.ppermute(tokens, ("yh", "zh"), QUARTER_TURN)
    own = jnp.transpose(feat_weight, (1, 0, 2))
    moved, late = lax.optimization_barrier((moved, own))
    weights = [own] + [
        lax.ppermute(part, X, [(i, i ^ away) for i in range(4)])
        for part, away in ((late, 1), (own, 2), (late, 3))
    ]
    pair_rows = jnp.stack([own, weights[3]])

    out_grad, short_taps, weights[2] = lax.optimization_barrier((out_grad, short_taps, weights[2]))
    grad_t, band = pl.pallas_call(
        prepare_kernel,
        out_shape=(
            jax.ShapeDtypeStruct((8, 16, HALF), BF16),
            jax.ShapeDtypeStruct((4, 128, 128), BF16),
        ),
        in_specs=[VMEM] * 2,
        out_specs=(VMEM,) * 2,
        name="prepare",
    )(out_grad, long_filter)
    table = pl.pallas_call(
        table_kernel,
        out_shape=jax.ShapeDtypeStruct((128, 128), F32),
        in_specs=[VMEM] * 2,
        out_specs=VMEM,
        cost_estimate=pl.CostEstimate(flops=20000000000, bytes_accessed=1 << 20, transcendentals=0),
        name="table",
    )(short_taps, skip_gain.reshape(1, 128))

    weights = [part.reshape(3, 4, 2, 128, 128) for part in weights]
    copies = pl.pallas_call(
        copies_kernel,
        out_shape=jax.ShapeDtypeStruct((32, 128, 128), BF16),
        in_specs=[VMEM],
        out_specs=VMEM,
        compiler_params=params(40),
        cost_estimate=pl.CostEstimate(flops=10000000000, bytes_accessed=1 << 20, transcendentals=0),
        name="copies",
    )(moved)
    whole = lax.all_to_all(copies, SPREAD, 0, 0, tiled=True).reshape(4, 2, 4, 128, 128)
    whole, grad_t, table, band, weights[1], pair_rows = lax.optimization_barrier(
        (whole, grad_t, table, band, weights[1], pair_rows)
    )
    w_z = lax.ppermute(pair_rows, "zp", pair).reshape(2, 3, 4, 2, 128, 128)
    across = lax.ppermute(whole, "core", pair)

    cost = pl.CostEstimate(flops=2 * 256 * 4096 * 384, bytes_accessed=5 << 20, transcendentals=0)
    mixed_shape = jax.ShapeDtypeStruct((8, ROWS, 128), BF16)
    partial = pl.pallas_call(
        project_kernel,
        out_shape=mixed_shape,
        in_specs=[VMEM] * 3 + [ANY] + [VMEM] * 3,
        out_specs=VMEM,
        scratch_shapes=[pltpu.VMEM((3, 4, 2, 128, 128), BF16), pltpu.SemaphoreType.DMA],
        compiler_params=params(40),
        cost_estimate=cost,
        name="project",
    )(whole, across, *weights, grad_t)
    spread = lax.all_to_all(partial, CTX, 0, 0, tiled=True)

    cotangent = pl.pallas_call(
        mixer_kernel,
        out_shape=jax.ShapeDtypeStruct((8, 2, ROWS, 128), BF16),
        in_specs=[VMEM] * 3,
        out_specs=VMEM,
        compiler_params=params(40),
        name="mixer",
    )(spread, table, band)
    gathered = lax.all_to_all(
        cotangent.reshape(16, ROWS, 128), RETURN, 0, 0, tiled=True
    ).reshape(8, 2, ROWS, 128)

    back_shape = jax.ShapeDtypeStruct((2, 2, 2, 2, 128, 128), BF16)
    back_own, back_other, filter_grad, small = pl.pallas_call(
        back_kernel,
        out_shape=(
            back_shape,
            back_shape,
            jax.ShapeDtypeStruct((8, 128), F32),
            jax.ShapeDtypeStruct((16, 128), F32),
        ),
        in_specs=[VMEM] * 3 + [ANY],
        out_specs=(VMEM,) * 4,
        scratch_shapes=[pltpu.VMEM((2, 3, 4, 2, 128, 128), BF16), pltpu.SemaphoreType.DMA((6,))],
        compiler_params=params(40),
        cost_estimate=cost,
        name="back",
    )(gathered, weights[0], weights[3], w_z)
    received = lax.ppermute(back_other, "core", pair)
    back = (back_own.astype(F32) + received.astype(F32)).astype(BF16)
    parts = lax.all_to_all(back.reshape(16, 128, 128), COLUMNS, 0, 0, tiled=True)
    summed = jnp.sum(parts.astype(F32), axis=0).astype(BF16)
    input_grad = lax.ppermute(summed, AXES, grad_route())
    return input_grad, filter_grad, small[9], small[:9].reshape(3, 3, 128)


def solution(mesh):
    split = Mesh(np.asarray(mesh.devices).reshape(SIZES), AXES)
    in_specs = (
        P(CTX, TP),
        P(CTX, None, TP),
        P(None, None, TP),
        P(TP, None),
        P(TP),
        P(CTX, TP),
    )
    out_specs = (P(CTX, TP), P(TP, None), P(TP), P(None, None, TP))
    return jax.shard_map(
        on_device, mesh=split, in_specs=in_specs, out_specs=out_specs, check_vma=False
    )
```

```python
import jax
import jax.numpy as jnp
import numpy as np
from jax import lax
from jax.experimental import pallas as pl
from jax.experimental.pallas import tpu as pltpu
from jax.sharding import Mesh
from jax.sharding import PartitionSpec as P

AXES = ("xh", "xl", "yh", "ylh", "yll", "zh", "z2", "zp", "core")
SIZES = (2,) * 9
X = ("xh", "xl")
CTX = ("xh", "xl", "yh")
TP = ("ylh", "yll", "zh", "z2", "zp", "core")
SPREAD = ("ylh", "yll", "zh", "z2", "zp")
RETURN = ("zp", "xh", "xl", "yh")
COLUMNS = ("ylh", "yll", "zh", "z2")
F32 = jnp.float32
BF16 = jnp.bfloat16
VMEM = pl.BlockSpec(memory_space=pltpu.VMEM)
ANY = pl.BlockSpec(memory_space=pl.ANY)
ROWS = 112
HALF = 128


def params(mib):
    return pltpu.CompilerParams(vmem_limit_bytes=mib * 1024 * 1024)


def rolled_rows(table, left):
    rows = lax.broadcasted_iota(jnp.int32, table.shape, 0)
    for bit in range(7):
        step = 1 << bit
        turned = pltpu.roll(table, 128 - step if left else step, 1)
        table = jnp.where((rows & step) != 0, turned, table)
    return table


def x_index():
    return 2 * lax.axis_index("xh") + lax.axis_index("xl")


def ctx_index():
    return 2 * x_index() + lax.axis_index("yh")


def block_place(away, z):
    high = lax.axis_index("xh") ^ away
    odd = lax.axis_index("xl") ^ lax.axis_index("zp") ^ away ^ 1
    return high, odd ^ (z % 2), z // 2


def copies_kernel(in_ref, out_ref):
    out_ref[...] = jnp.broadcast_to(in_ref[...][None], (32, 128, 128))


def table_kernel(taps_ref, skip_ref, table_ref):
    rows = jnp.concatenate(
        [taps_ref[0], taps_ref[1], taps_ref[2], skip_ref[...], jnp.zeros((118, 128), F32)], axis=0
    )
    table_ref[...] = rows.T


def prepare_kernel(grad_ref, filter_ref, grad_t_ref, band_ref):
    grad_t_ref[...] = grad_ref[...].astype(F32).T.astype(BF16).reshape(8, 16, HALF)
    band = rolled_rows(
        jnp.broadcast_to(filter_ref[pl.ds(ctx_index(), 1), :], (128, 128)), False
    )
    src = lax.broadcasted_iota(jnp.int32, (128, 128), 0)
    dst = lax.broadcasted_iota(jnp.int32, (128, 128), 1)
    near = jnp.where(dst >= src, band, 0.0)
    far = jnp.where(dst < src, band, 0.0)
    for place_at, part in ((0, near), (2, far)):
        high = part.astype(BF16)
        band_ref[place_at] = high
        band_ref[place_at + 1] = (part - high.astype(F32)).astype(BF16)


def arrived_kernel(in_ref, out_ref, tile, sem):
    del out_ref
    copy = pltpu.make_async_copy(in_ref.at[0, 0, 0, 0], tile, sem)
    copy.start()
    copy.wait()


def arrived(weight):
    return pl.pallas_call(
        arrived_kernel,
        out_shape=jax.ShapeDtypeStruct(weight.shape, weight.dtype),
        in_specs=[ANY],
        out_specs=ANY,
        input_output_aliases={0: 0},
        scratch_shapes=[pltpu.VMEM((128, 128), BF16), pltpu.SemaphoreType.DMA],
        cost_estimate=pl.CostEstimate(flops=20000000000, bytes_accessed=1 << 16, transcendentals=0),
        name="arrived",
    )(weight)


def weight_rows(weight, proj, side):
    return jnp.concatenate([weight[proj, z, side] for z in range(4)], axis=0)


def project_kernel(own_ref, other_ref, w0, w1, w2_late, w3, grad_ref, out_ref, w2, sem, grad_sems):
    copy = pltpu.make_async_copy(w2_late, w2, sem)
    copy.start()
    grads = [
        pltpu.make_async_copy(grad_ref.at[k], out_ref.at[k, 96:ROWS], grad_sems.at[k])
        for k in range(8)
    ]
    for grad in grads:
        grad.start()
    x = x_index()
    core = lax.axis_index("core")
    totals = [jnp.zeros((256, 128), F32) for _ in range(3)]
    for away, weight in ((0, w0), (1, w1), (3, w3), (2, w2)):
        if away == 2:
            copy.wait()
        block = x ^ away
        for ref, side in ((own_ref, core), (other_ref, 1 - core)):
            rows = jnp.concatenate(
                [
                    jnp.concatenate([ref[block, 1 - half, z] for z in range(4)], axis=1)
                    for half in range(2)
                ],
                axis=0,
            )
            for proj in range(3):
                totals[proj] = totals[proj] + jnp.dot(
                    rows, weight_rows(weight, proj, side), preferred_element_type=F32
                )
    for proj in range(3):
        turned = totals[proj].T.astype(BF16)
        for half in range(2):
            start = (2 * proj + half) * 16
            for group in range(8):
                out_ref[group, start : start + 16, :] = turned[
                    group * 16 : group * 16 + 16, half * 128 : half * 128 + 128
                ]
    for grad in grads:
        grad.wait()


def mixer_kernel(in_ref, table_ref, band_ref, out_ref):
    ctx = ctx_index()
    tokens = 1024
    lane = lax.broadcasted_iota(jnp.int32, (16, tokens), 1)
    table = table_ref[pl.ds(pl.multiple_of(ctx * 16, 16), 16), :]

    def column(k):
        return table[:, k : k + 1]

    def behind(block, k):
        if k == 0:
            return block
        return jnp.where(lane >= k, pltpu.roll(block, k, 1), 0.0)

    def ahead(block, k):
        if k == 0:
            return block
        return jnp.where(lane < tokens - k, pltpu.roll(block, tokens - k, 1), 0.0)

    def stacked(block):
        return jnp.concatenate([block[:, 128 * b : 128 * b + 128] for b in range(8)], axis=0)

    def flat(block):
        return jnp.concatenate([block[16 * b : 16 * b + 16] for b in range(8)], axis=1)

    grad_out = jnp.concatenate(
        [in_ref[i, 96:ROWS, :] for i in range(8)], axis=1
    ).astype(F32)
    feats = []
    mixed = []
    for proj in range(3):
        pieces = []
        for x in range(4):
            for half in range(2):
                start = (2 * proj + half) * 16
                pieces.append(
                    in_ref[2 * x, start : start + 16, :].astype(F32)
                    + in_ref[2 * x + 1, start : start + 16, :].astype(F32)
                )
        feat = jnp.concatenate(pieces, axis=1).astype(BF16).astype(F32)
        shifted = [behind(feat, k) for k in range(3)]
        feats.append(shifted)
        running = jnp.zeros((16, tokens), F32)
        for k in range(3):
            running = running + column(3 * k + proj) * shifted[k]
        mixed.append(running)
    query, key, value = mixed
    skip = column(9)
    product = (key * value).astype(BF16)
    dconv = (grad_out * query).astype(BF16)
    prod_rows = stacked(product)
    conv_rows = stacked(dconv)
    none = jnp.zeros((16, 128), BF16)
    prod_prev = jnp.concatenate([none, prod_rows[:112]], axis=0)
    conv_next = jnp.concatenate([conv_rows[16:], none], axis=0)
    forward = jnp.zeros((128, 128), F32)
    backward = jnp.zeros((128, 128), F32)
    over_last = (((1,), (1,)), ((), ()))
    over_first = (((0,), (0,)), ((), ()))
    for at, (left, right) in enumerate(
        ((prod_rows, conv_rows), (prod_rows, conv_rows), (prod_prev, conv_next), (prod_prev, conv_next))
    ):
        band = band_ref[at]
        forward = forward + jnp.dot(left, band, preferred_element_type=F32)
        backward = backward + lax.dot_general(right, band, over_last, preferred_element_type=F32)
    product_f = product.astype(F32)
    dconv_f = dconv.astype(F32)
    long_conv = flat(forward) + skip * product_f
    dproduct = flat(backward) + skip * dconv_f
    near = lax.dot_general(prod_rows, conv_rows, over_first, preferred_element_type=F32)
    far = lax.dot_general(prod_prev, conv_rows, over_first, preferred_element_type=F32)
    src = lax.broadcasted_iota(jnp.int32, (128, 128), 0)
    dst = lax.broadcasted_iota(jnp.int32, (128, 128), 1)
    cross = rolled_rows(jnp.where(dst >= src, near, far), True)
    filter_grad = jnp.sum(cross, axis=0, keepdims=True)
    skip_grad = jnp.sum(dconv_f * product_f, axis=1, keepdims=True)
    dmixed = (grad_out * long_conv, dproduct * value, dproduct * key)
    row16 = lax.broadcasted_iota(jnp.int32, (16, 128), 0)
    lane16 = lax.broadcasted_iota(jnp.int32, (16, 128), 1)
    small = jnp.where((lane16 & 15) == 9, skip_grad, 0.0)
    for proj in range(3):
        dfeat = jnp.zeros((16, tokens), F32)
        for k in range(3):
            dfeat = dfeat + column(3 * k + proj) * ahead(dmixed[proj], k)
            short = jnp.sum(dmixed[proj] * feats[proj][k], axis=1, keepdims=True)
            small = jnp.where((lane16 & 15) == 3 * k + proj, short, small)
        dfeat = dfeat.astype(BF16)
        for ctx_to in range(8):
            xh, xl = ctx_to // 4, ctx_to // 2 % 2
            for zp in range(2):
                for yh in range(2):
                    piece = 128 * (4 * xh + 2 * (zp ^ xl) + yh)
                    start = (2 * proj + yh) * 16
                    out_ref[zp, ctx_to, start : start + 16, :] = dfeat[:, piece : piece + 128]
    small_high = small.astype(BF16).astype(F32)
    small_both = jnp.where(lane16 < 16, small_high, small - small_high)
    filter_high = filter_grad.astype(BF16).astype(F32)
    filter_low = filter_grad - filter_high
    extra = jnp.where(lane16 < 32, small_both, 0.0)
    for at, (part, shift) in enumerate(
        ((filter_high, 0), (filter_low, 0), (filter_high, 32), (filter_low, 32))
    ):
        line = jnp.broadcast_to(part, (16, 128))
        if shift:
            line = pltpu.roll(line, shift, 1)
        extra = jnp.where((row16 == at) & (lane16 >= 32), line, extra)
    extra = extra.astype(BF16)
    for i in range(8):
        for zp in range(2):
            out_ref[zp, i, 96:ROWS, :] = extra


def back_kernel(
    in_ref, w_own, w_x, w_far, own_ref, other_ref, filter_ref, small_ref, w_z, sems
):
    copies = [
        pltpu.make_async_copy(w_far.at[k // 3, k % 3], w_z.at[k // 3, k % 3], sems.at[k])
        for k in range(6)
    ]
    for copy in copies:
        copy.start()
    zp = lax.axis_index("zp")
    core = lax.axis_index("core")
    weights = ((w_own, w_z.at[0]), (w_x, w_z.at[1]))
    halves = []
    for half in range(2):
        columns = []
        for over in range(2):
            of_z = zp ^ over
            for proj in range(3):
                start = (2 * proj + half) * 16
                block = jnp.concatenate(
                    [in_ref[of_z, i, start : start + 16, :] for i in range(8)], axis=0
                )
                columns.append(block.astype(F32).T.astype(BF16))
        halves.append(jnp.concatenate(columns, axis=1))
    rows = jnp.concatenate(halves, axis=0)
    for away in range(2):
        for copy in copies[3 * away : 3 * away + 3]:
            copy.wait()
        for ref, side in ((own_ref, core), (other_ref, 1 - core)):
            table = jnp.concatenate(
                [
                    weight_rows(weight, proj, side)
                    for weight in weights[away]
                    for proj in range(3)
                ],
                axis=1,
            )
            result = lax.dot_general(
                rows, table, (((1,), (1,)), ((), ())), preferred_element_type=F32
            ).astype(BF16)
            for half in range(2):
                for z in range(4):
                    high, low, z2 = block_place(away, z)
                    ref[high, low, 1 - half, z2] = result[
                        half * 128 : half * 128 + 128, z * 128 : z * 128 + 128
                    ]
    extra = [in_ref[zp, i, 96:ROWS, :].astype(F32) for i in range(8)]
    turned = jnp.concatenate(extra, axis=0).T
    small_ref[...] = turned[0:16] + turned[16:32]
    lane = lax.broadcasted_iota(jnp.int32, (1, 128), 1)
    for i in range(8):
        late = extra[i][0:1] + extra[i][1:2]
        early = extra[i][2:3] + extra[i][3:4]
        early = pltpu.roll(jnp.broadcast_to(early, (8, 128)), 96, 1)[0:1]
        filter_ref[i : i + 1, :] = jnp.where(lane < 32, early, late)


QUARTER_TURN = [(0, 1), (1, 3), (2, 0), (3, 2)]


def flat_index(bits):
    at = 0
    for bit in bits:
        at = 2 * at + bit
    return at


def grad_route():
    route = []
    for xh, xl, yh, ylh, yll, zh, z2, zp, c in np.ndindex(SIZES):
        source = flat_index((xh, xl, yh, ylh, yll, zh, z2, zp, c))
        low = xh ^ ylh ^ yll
        moved = low ^ xl
        target = flat_index((xh, low, zh, ylh, yll ^ zp ^ moved ^ 1, 1 - yh, z2, moved, c))
        route.append((target, source))
    return route


def on_device(tokens, feat_weight, short_taps, long_filter, skip_gain, out_grad):
    pair = [(0, 1), (1, 0)]
    moved = lax.ppermute(tokens, ("yh", "zh"), QUARTER_TURN)
    own = jnp.transpose(feat_weight, (1, 0, 2))
    moved, late = lax.optimization_barrier((moved, own))
    weights = [own] + [
        lax.ppermute(part, X, [(i, i ^ away) for i in range(4)])
        for part, away in ((own, 1), (late, 2), (own, 3))
    ]
    pair_rows = jnp.stack([own, weights[3]])

    out_grad, short_taps, weights[1], weights[3] = lax.optimization_barrier(
        (out_grad, short_taps, weights[1], weights[3])
    )
    grad_t, band = pl.pallas_call(
        prepare_kernel,
        out_shape=(
            jax.ShapeDtypeStruct((8, 16, HALF), BF16),
            jax.ShapeDtypeStruct((4, 128, 128), BF16),
        ),
        in_specs=[VMEM] * 2,
        out_specs=(VMEM,) * 2,
        name="prepare",
    )(out_grad, long_filter)
    table = pl.pallas_call(
        table_kernel,
        out_shape=jax.ShapeDtypeStruct((128, 128), F32),
        in_specs=[VMEM] * 2,
        out_specs=VMEM,
        cost_estimate=pl.CostEstimate(flops=20000000000, bytes_accessed=1 << 20, transcendentals=0),
        name="table",
    )(short_taps, skip_gain.reshape(1, 128))

    weights = [part.reshape(3, 4, 2, 128, 128) for part in weights]
    copies = pl.pallas_call(
        copies_kernel,
        out_shape=jax.ShapeDtypeStruct((32, 128, 128), BF16),
        in_specs=[VMEM],
        out_specs=VMEM,
        compiler_params=params(40),
        cost_estimate=pl.CostEstimate(flops=10000000000, bytes_accessed=1 << 20, transcendentals=0),
        name="copies",
    )(moved)
    whole = lax.all_to_all(copies, SPREAD, 0, 0, tiled=True).reshape(4, 2, 4, 128, 128)
    w_z = lax.ppermute(pair_rows, "zp", pair).reshape(2, 3, 4, 2, 128, 128)
    whole, grad_t, table, band, weights[2] = lax.optimization_barrier(
        (whole, grad_t, table, band, weights[2])
    )
    across = lax.ppermute(whole, "core", pair)

    cost = pl.CostEstimate(flops=2 * 256 * 4096 * 384, bytes_accessed=5 << 20, transcendentals=0)
    mixed_shape = jax.ShapeDtypeStruct((8, ROWS, 128), BF16)
    partial = pl.pallas_call(
        project_kernel,
        out_shape=mixed_shape,
        in_specs=[VMEM] * 4 + [ANY, VMEM, ANY],
        out_specs=VMEM,
        scratch_shapes=[
            pltpu.VMEM((3, 4, 2, 128, 128), BF16),
            pltpu.SemaphoreType.DMA,
            pltpu.SemaphoreType.DMA((8,)),
        ],
        compiler_params=params(40),
        cost_estimate=cost,
        name="project",
    )(whole, across, *weights, grad_t)
    spread = lax.all_to_all(partial, CTX, 0, 0, tiled=True)

    cotangent = pl.pallas_call(
        mixer_kernel,
        out_shape=jax.ShapeDtypeStruct((2, 8, ROWS, 128), BF16),
        in_specs=[VMEM] * 3,
        out_specs=VMEM,
        compiler_params=params(40),
        name="mixer",
    )(spread, table, band)
    gathered = lax.all_to_all(
        cotangent.reshape(16, ROWS, 128), RETURN, 0, 0, tiled=True
    ).reshape(2, 8, ROWS, 128)

    back_shape = jax.ShapeDtypeStruct((2, 2, 2, 2, 128, 128), BF16)
    back_own, back_other, filter_grad, small = pl.pallas_call(
        back_kernel,
        out_shape=(
            back_shape,
            back_shape,
            jax.ShapeDtypeStruct((8, 128), F32),
            jax.ShapeDtypeStruct((16, 128), F32),
        ),
        in_specs=[VMEM] * 3 + [ANY],
        out_specs=(VMEM,) * 4,
        scratch_shapes=[pltpu.VMEM((2, 3, 4, 2, 128, 128), BF16), pltpu.SemaphoreType.DMA((6,))],
        compiler_params=params(40),
        cost_estimate=cost,
        name="back",
    )(gathered, weights[0], weights[3], arrived(w_z))
    received = lax.ppermute(back_other, "core", pair)
    back = (back_own.astype(F32) + received.astype(F32)).astype(BF16)
    parts = lax.all_to_all(back.reshape(16, 128, 128), COLUMNS, 0, 0, tiled=True)
    summed = jnp.sum(parts.astype(F32), axis=0).astype(BF16)
    input_grad = lax.ppermute(summed, AXES, grad_route())
    return input_grad, filter_grad, small[9], small[:9].reshape(3, 3, 128)


def solution(mesh):
    split = Mesh(np.asarray(mesh.devices).reshape(SIZES), AXES)
    in_specs = (
        P(CTX, TP),
        P(CTX, None, TP),
        P(None, None, TP),
        P(TP, None),
        P(TP),
        P(CTX, TP),
    )
    out_specs = (P(CTX, TP), P(TP, None), P(TP), P(None, None, TP))
    return jax.shard_map(
        on_device, mesh=split, in_specs=in_specs, out_specs=out_specs, check_vma=False
    )
```

```python
import jax
import jax.numpy as jnp
import numpy as np
from jax import lax
from jax.experimental import pallas as pl
from jax.experimental.pallas import tpu as pltpu
from jax.sharding import Mesh
from jax.sharding import PartitionSpec as P

AXES = ("xh", "xl", "yh", "ylh", "yll", "zh", "z2", "zp", "core")
SIZES = (2,) * 9
X = ("xh", "xl")
CTX = ("xh", "xl", "yh")
TP = ("ylh", "yll", "zh", "z2", "zp", "core")
SPREAD = ("ylh", "yll", "zh", "z2", "zp")
RETURN = ("zp", "xh", "xl", "yh")
COLUMNS = ("ylh", "yll", "zh", "z2")
F32 = jnp.float32
BF16 = jnp.bfloat16
VMEM = pl.BlockSpec(memory_space=pltpu.VMEM)
ANY = pl.BlockSpec(memory_space=pl.ANY)
ROWS = 112
HALF = 128


def params(mib):
    return pltpu.CompilerParams(vmem_limit_bytes=mib * 1024 * 1024)


def rolled_rows(table, left):
    rows = lax.broadcasted_iota(jnp.int32, table.shape, 0)
    for bit in range(7):
        step = 1 << bit
        turned = pltpu.roll(table, 128 - step if left else step, 1)
        table = jnp.where((rows & step) != 0, turned, table)
    return table


def x_index():
    return 2 * lax.axis_index("xh") + lax.axis_index("xl")


def ctx_index():
    return 2 * x_index() + lax.axis_index("yh")


def block_place(away, z):
    high = lax.axis_index("xh") ^ away
    odd = lax.axis_index("xl") ^ lax.axis_index("zp") ^ away ^ 1
    return high, odd ^ (z % 2), z // 2


def copies_kernel(in_ref, out_ref):
    out_ref[...] = jnp.broadcast_to(in_ref[...][None], (32, 128, 128))


def table_kernel(taps_ref, skip_ref, table_ref):
    rows = jnp.concatenate(
        [taps_ref[0], taps_ref[1], taps_ref[2], skip_ref[...], jnp.zeros((118, 128), F32)], axis=0
    )
    table_ref[...] = rows.T


def prepare_kernel(filter_ref, band_ref):
    band = rolled_rows(
        jnp.broadcast_to(filter_ref[pl.ds(ctx_index(), 1), :], (128, 128)), False
    )
    src = lax.broadcasted_iota(jnp.int32, (128, 128), 0)
    dst = lax.broadcasted_iota(jnp.int32, (128, 128), 1)
    near = jnp.where(dst >= src, band, 0.0)
    far = jnp.where(dst < src, band, 0.0)
    for place_at, part in ((0, near), (2, far)):
        high = part.astype(BF16)
        band_ref[place_at] = high
        band_ref[place_at + 1] = (part - high.astype(F32)).astype(BF16)


def arrived_kernel(in_ref, out_ref, tile, sem):
    del out_ref
    copy = pltpu.make_async_copy(in_ref.at[0, 0, 0, 0], tile, sem)
    copy.start()
    copy.wait()


def arrived(weight):
    return pl.pallas_call(
        arrived_kernel,
        out_shape=jax.ShapeDtypeStruct(weight.shape, weight.dtype),
        in_specs=[ANY],
        out_specs=ANY,
        input_output_aliases={0: 0},
        scratch_shapes=[pltpu.VMEM((128, 128), BF16), pltpu.SemaphoreType.DMA],
        cost_estimate=pl.CostEstimate(flops=20000000000, bytes_accessed=1 << 16, transcendentals=0),
        name="arrived",
    )(weight)


def weight_rows(weight, proj, side):
    return jnp.concatenate([weight[proj, z, side] for z in range(4)], axis=0)


def project_kernel(own_ref, other_ref, w0, w1, w2_late, w3, grad_ref, out_ref, w2, sem):
    copy = pltpu.make_async_copy(w2_late, w2, sem)
    copy.start()
    x = x_index()
    core = lax.axis_index("core")
    totals = [jnp.zeros((256, 128), F32) for _ in range(3)]
    for away, weight in ((0, w0), (1, w1), (3, w3), (2, w2)):
        if away == 2:
            copy.wait()
        block = x ^ away
        for ref, side in ((own_ref, core), (other_ref, 1 - core)):
            rows = jnp.concatenate(
                [
                    jnp.concatenate([ref[block, 1 - half, z] for z in range(4)], axis=1)
                    for half in range(2)
                ],
                axis=0,
            )
            for proj in range(3):
                totals[proj] = totals[proj] + jnp.dot(
                    rows, weight_rows(weight, proj, side), preferred_element_type=F32
                )
    for proj in range(3):
        turned = totals[proj].T.astype(BF16)
        for half in range(2):
            start = (2 * proj + half) * 16
            for group in range(8):
                out_ref[group, start : start + 16, :] = turned[
                    group * 16 : group * 16 + 16, half * 128 : half * 128 + 128
                ]
    turned = grad_ref[...].astype(F32).T.astype(BF16)
    for group in range(8):
        out_ref[group, 96:ROWS, :] = turned[group * 16 : group * 16 + 16]


def mixer_kernel(in_ref, table_ref, band_ref, out_ref):
    ctx = ctx_index()
    tokens = 1024
    lane = lax.broadcasted_iota(jnp.int32, (16, tokens), 1)
    table = table_ref[pl.ds(pl.multiple_of(ctx * 16, 16), 16), :]

    def column(k):
        return table[:, k : k + 1]

    def behind(block, k):
        if k == 0:
            return block
        return jnp.where(lane >= k, pltpu.roll(block, k, 1), 0.0)

    def ahead(block, k):
        if k == 0:
            return block
        return jnp.where(lane < tokens - k, pltpu.roll(block, tokens - k, 1), 0.0)

    def stacked(block):
        return jnp.concatenate([block[:, 128 * b : 128 * b + 128] for b in range(8)], axis=0)

    def flat(block):
        return jnp.concatenate([block[16 * b : 16 * b + 16] for b in range(8)], axis=1)

    grad_out = jnp.concatenate(
        [in_ref[i, 96:ROWS, :] for i in range(8)], axis=1
    ).astype(F32)
    feats = []
    mixed = []
    for proj in range(3):
        pieces = []
        for x in range(4):
            for half in range(2):
                start = (2 * proj + half) * 16
                pieces.append(
                    in_ref[2 * x, start : start + 16, :].astype(F32)
                    + in_ref[2 * x + 1, start : start + 16, :].astype(F32)
                )
        feat = jnp.concatenate(pieces, axis=1).astype(BF16).astype(F32)
        shifted = [behind(feat, k) for k in range(3)]
        feats.append(shifted)
        running = jnp.zeros((16, tokens), F32)
        for k in range(3):
            running = running + column(3 * k + proj) * shifted[k]
        mixed.append(running)
    query, key, value = mixed
    skip = column(9)
    product = (key * value).astype(BF16)
    dconv = (grad_out * query).astype(BF16)
    prod_rows = stacked(product)
    conv_rows = stacked(dconv)
    none = jnp.zeros((16, 128), BF16)
    prod_prev = jnp.concatenate([none, prod_rows[:112]], axis=0)
    conv_next = jnp.concatenate([conv_rows[16:], none], axis=0)
    forward = jnp.zeros((128, 128), F32)
    backward = jnp.zeros((128, 128), F32)
    over_last = (((1,), (1,)), ((), ()))
    over_first = (((0,), (0,)), ((), ()))
    for at, (left, right) in enumerate(
        ((prod_rows, conv_rows), (prod_rows, conv_rows), (prod_prev, conv_next), (prod_prev, conv_next))
    ):
        band = band_ref[at]
        forward = forward + jnp.dot(left, band, preferred_element_type=F32)
        backward = backward + lax.dot_general(right, band, over_last, preferred_element_type=F32)
    product_f = product.astype(F32)
    dconv_f = dconv.astype(F32)
    long_conv = flat(forward) + skip * product_f
    dproduct = flat(backward) + skip * dconv_f
    near = lax.dot_general(prod_rows, conv_rows, over_first, preferred_element_type=F32)
    far = lax.dot_general(prod_prev, conv_rows, over_first, preferred_element_type=F32)
    src = lax.broadcasted_iota(jnp.int32, (128, 128), 0)
    dst = lax.broadcasted_iota(jnp.int32, (128, 128), 1)
    cross = rolled_rows(jnp.where(dst >= src, near, far), True)
    filter_grad = jnp.sum(cross, axis=0, keepdims=True)
    skip_grad = jnp.sum(dconv_f * product_f, axis=1, keepdims=True)
    dmixed = (grad_out * long_conv, dproduct * value, dproduct * key)
    row16 = lax.broadcasted_iota(jnp.int32, (16, 128), 0)
    lane16 = lax.broadcasted_iota(jnp.int32, (16, 128), 1)
    small = jnp.where((lane16 & 15) == 9, skip_grad, 0.0)
    for proj in range(3):
        dfeat = jnp.zeros((16, tokens), F32)
        for k in range(3):
            dfeat = dfeat + column(3 * k + proj) * ahead(dmixed[proj], k)
            short = jnp.sum(dmixed[proj] * feats[proj][k], axis=1, keepdims=True)
            small = jnp.where((lane16 & 15) == 3 * k + proj, short, small)
        dfeat = dfeat.astype(BF16)
        for ctx_to in range(8):
            xh, xl = ctx_to // 4, ctx_to // 2 % 2
            for zp in range(2):
                for yh in range(2):
                    piece = 128 * (4 * xh + 2 * (zp ^ xl) + yh)
                    start = (2 * proj + yh) * 16
                    out_ref[zp, ctx_to, start : start + 16, :] = dfeat[:, piece : piece + 128]
    small_high = small.astype(BF16).astype(F32)
    small_both = jnp.where(lane16 < 16, small_high, small - small_high)
    filter_high = filter_grad.astype(BF16).astype(F32)
    filter_low = filter_grad - filter_high
    extra = jnp.where(lane16 < 32, small_both, 0.0)
    for at, (part, shift) in enumerate(
        ((filter_high, 0), (filter_low, 0), (filter_high, 32), (filter_low, 32))
    ):
        line = jnp.broadcast_to(part, (16, 128))
        if shift:
            line = pltpu.roll(line, shift, 1)
        extra = jnp.where((row16 == at) & (lane16 >= 32), line, extra)
    extra = extra.astype(BF16)
    for i in range(8):
        for zp in range(2):
            out_ref[zp, i, 96:ROWS, :] = extra


def back_kernel(
    in_ref, w_own, w_x, w_far, own_ref, other_ref, filter_ref, small_ref, w_z, sems
):
    copies = [
        pltpu.make_async_copy(w_far.at[k // 3, k % 3], w_z.at[k // 3, k % 3], sems.at[k])
        for k in range(6)
    ]
    for copy in copies:
        copy.start()
    zp = lax.axis_index("zp")
    core = lax.axis_index("core")
    weights = ((w_own, w_z.at[0]), (w_x, w_z.at[1]))
    halves = []
    for half in range(2):
        columns = []
        for over in range(2):
            of_z = zp ^ over
            for proj in range(3):
                start = (2 * proj + half) * 16
                block = jnp.concatenate(
                    [in_ref[of_z, i, start : start + 16, :] for i in range(8)], axis=0
                )
                columns.append(block.astype(F32).T.astype(BF16))
        halves.append(jnp.concatenate(columns, axis=1))
    rows = jnp.concatenate(halves, axis=0)
    for away in range(2):
        for copy in copies[3 * away : 3 * away + 3]:
            copy.wait()
        for ref, side in ((own_ref, core), (other_ref, 1 - core)):
            table = jnp.concatenate(
                [
                    weight_rows(weight, proj, side)
                    for weight in weights[away]
                    for proj in range(3)
                ],
                axis=1,
            )
            result = lax.dot_general(
                rows, table, (((1,), (1,)), ((), ())), preferred_element_type=F32
            ).astype(BF16)
            for half in range(2):
                for z in range(4):
                    high, low, z2 = block_place(away, z)
                    ref[high, low, 1 - half, z2] = result[
                        half * 128 : half * 128 + 128, z * 128 : z * 128 + 128
                    ]
    extra = [in_ref[zp, i, 96:ROWS, :].astype(F32) for i in range(8)]
    turned = jnp.concatenate(extra, axis=0).T
    small_ref[...] = turned[0:16] + turned[16:32]
    lane = lax.broadcasted_iota(jnp.int32, (1, 128), 1)
    for i in range(8):
        late = extra[i][0:1] + extra[i][1:2]
        early = extra[i][2:3] + extra[i][3:4]
        early = pltpu.roll(jnp.broadcast_to(early, (8, 128)), 96, 1)[0:1]
        filter_ref[i : i + 1, :] = jnp.where(lane < 32, early, late)


QUARTER_TURN = [(0, 1), (1, 3), (2, 0), (3, 2)]


def flat_index(bits):
    at = 0
    for bit in bits:
        at = 2 * at + bit
    return at


def grad_route():
    route = []
    for xh, xl, yh, ylh, yll, zh, z2, zp, c in np.ndindex(SIZES):
        source = flat_index((xh, xl, yh, ylh, yll, zh, z2, zp, c))
        low = xh ^ ylh ^ yll
        moved = low ^ xl
        target = flat_index((xh, low, zh, ylh, yll ^ zp ^ moved ^ 1, 1 - yh, z2, moved, c))
        route.append((target, source))
    return route


def on_device(tokens, feat_weight, short_taps, long_filter, skip_gain, out_grad):
    pair = [(0, 1), (1, 0)]
    moved = lax.ppermute(tokens, ("yh", "zh"), QUARTER_TURN)
    own = jnp.transpose(feat_weight, (1, 0, 2))
    moved, late = lax.optimization_barrier((moved, own))
    weights = [own] + [
        lax.ppermute(part, X, [(i, i ^ away) for i in range(4)])
        for part, away in ((own, 1), (late, 2), (own, 3))
    ]
    pair_rows = jnp.stack([own, weights[3]])

    long_filter, short_taps, weights[1], weights[3] = lax.optimization_barrier(
        (long_filter, short_taps, weights[1], weights[3])
    )
    band = pl.pallas_call(
        prepare_kernel,
        out_shape=jax.ShapeDtypeStruct((4, 128, 128), BF16),
        in_specs=[VMEM],
        out_specs=VMEM,
        name="prepare",
    )(long_filter)
    table = pl.pallas_call(
        table_kernel,
        out_shape=jax.ShapeDtypeStruct((128, 128), F32),
        in_specs=[VMEM] * 2,
        out_specs=VMEM,
        cost_estimate=pl.CostEstimate(flops=20000000000, bytes_accessed=1 << 20, transcendentals=0),
        name="table",
    )(short_taps, skip_gain.reshape(1, 128))

    weights = [part.reshape(3, 4, 2, 128, 128) for part in weights]
    copies = pl.pallas_call(
        copies_kernel,
        out_shape=jax.ShapeDtypeStruct((32, 128, 128), BF16),
        in_specs=[VMEM],
        out_specs=VMEM,
        compiler_params=params(40),
        cost_estimate=pl.CostEstimate(flops=10000000000, bytes_accessed=1 << 20, transcendentals=0),
        name="copies",
    )(moved)
    whole = lax.all_to_all(copies, SPREAD, 0, 0, tiled=True).reshape(4, 2, 4, 128, 128)
    w_z = lax.ppermute(pair_rows, "zp", pair).reshape(2, 3, 4, 2, 128, 128)
    whole, table, band, weights[2] = lax.optimization_barrier((whole, table, band, weights[2]))
    across = lax.ppermute(whole, "core", pair)

    cost = pl.CostEstimate(flops=2 * 256 * 4096 * 384, bytes_accessed=5 << 20, transcendentals=0)
    mixed_shape = jax.ShapeDtypeStruct((8, ROWS, 128), BF16)
    partial = pl.pallas_call(
        project_kernel,
        out_shape=mixed_shape,
        in_specs=[VMEM] * 4 + [ANY, VMEM, VMEM],
        out_specs=VMEM,
        scratch_shapes=[
            pltpu.VMEM((3, 4, 2, 128, 128), BF16),
            pltpu.SemaphoreType.DMA,
        ],
        compiler_params=params(40),
        cost_estimate=cost,
        name="project",
    )(whole, across, *weights, out_grad)
    spread = lax.all_to_all(partial, CTX, 0, 0, tiled=True)

    cotangent = pl.pallas_call(
        mixer_kernel,
        out_shape=jax.ShapeDtypeStruct((2, 8, ROWS, 128), BF16),
        in_specs=[VMEM] * 3,
        out_specs=VMEM,
        compiler_params=params(40),
        name="mixer",
    )(spread, table, band)
    gathered = lax.all_to_all(
        cotangent.reshape(16, ROWS, 128), RETURN, 0, 0, tiled=True
    ).reshape(2, 8, ROWS, 128)

    back_shape = jax.ShapeDtypeStruct((2, 2, 2, 2, 128, 128), BF16)
    back_own, back_other, filter_grad, small = pl.pallas_call(
        back_kernel,
        out_shape=(
            back_shape,
            back_shape,
            jax.ShapeDtypeStruct((8, 128), F32),
            jax.ShapeDtypeStruct((16, 128), F32),
        ),
        in_specs=[VMEM] * 3 + [ANY],
        out_specs=(VMEM,) * 4,
        scratch_shapes=[pltpu.VMEM((2, 3, 4, 2, 128, 128), BF16), pltpu.SemaphoreType.DMA((6,))],
        compiler_params=params(40),
        cost_estimate=cost,
        name="back",
    )(gathered, weights[0], weights[3], arrived(w_z))
    received = lax.ppermute(back_other, "core", pair)
    back = (back_own.astype(F32) + received.astype(F32)).astype(BF16)
    parts = lax.all_to_all(back.reshape(16, 128, 128), COLUMNS, 0, 0, tiled=True)
    summed = jnp.sum(parts.astype(F32), axis=0).astype(BF16)
    input_grad = lax.ppermute(summed, AXES, grad_route())
    return input_grad, filter_grad, small[9], small[:9].reshape(3, 3, 128)


def solution(mesh):
    split = Mesh(np.asarray(mesh.devices).reshape(SIZES), AXES)
    in_specs = (
        P(CTX, TP),
        P(CTX, None, TP),
        P(None, None, TP),
        P(TP, None),
        P(TP),
        P(CTX, TP),
    )
    out_specs = (P(CTX, TP), P(TP, None), P(TP), P(None, None, TP))
    return jax.shard_map(
        on_device, mesh=split, in_specs=in_specs, out_specs=out_specs, check_vma=False
    )
```
